32 devices in a mesh: wave: 8 (over y, x, core), lev: 4 (over z).
Axes of the slice: x: 2, y: 2, z: 4, core: 2. Of those that a mesh axis runs over, the one named last changes fastest.
Arguments:
- vort_div: float32 [4, 4, 80, 80], P(None, 'lev', 'wave'), may hold values from -0.4 to 0.4
- legendre: float32 [80, 8, 80], P('wave'), may hold values from -1 to 1
- owner_map: int32 [80], replicated, may hold values from 0 to 79, as said below
- lat_sine: float32 [8], P('wave'), may hold values from -0.9 to 0.9
- quad_weight: float32 [8], P('wave'), may hold values from 2 to 6
- thickness: float32 [4], P('lev'), may hold values from 0.02 to 0.08
- tracers: float32 [8, 4, 8, 160], P(None, 'lev', 'wave'), may hold values from -6 to 6
Outputs:
- tendency: float32 [8, 2, 4, 80, 80], P(None, None, 'lev', 'wave')
The draws below stay inside these ranges and needn't reach their ends.
Inputs may be any that keep to these rules, and one draw needn't show every extreme that they name: `owner_map`: a permutation of the 80 wavenumbers in which slots 2 i and 2 i + 1 hold m and 79 - m.
All inputs are finite; a program needn't handle non-finite values.
Results may differ from the reference program's by a relative error of at most 0.00007.
Values sent between devices are 32-bit elements; how exact they have to be, the bound alone decides.
A program may use at most 64 MiB of HBM per device.

```python
import math
import jax
import jax.numpy as jnp
from jax import lax

M = 80
NLON = 160
LATS = 8
LEVELS = 4
TRACERS = 8


def draw_owner_map(key, part):
    shuffled = jax.random.permutation(jax.random.fold_in(key, 17), M // 2)
    paired = jnp.stack([shuffled, M - 1 - shuffled], axis=1).reshape(-1)
    return paired.astype(jnp.int32)


def level_of(stream_key, dims, cuts, low, top_value):
    factor_of, own = 1.0, jax.random.fold_in(stream_key, 6)
    for axis_at, parts in cuts:
        draws = jnp.exp(jax.random.uniform(jax.random.fold_in(own, axis_at), (parts,), jnp.float32, low / len(cuts), top_value / len(cuts)))
        factor_of = factor_of * jnp.repeat(draws, dims[axis_at] // parts).reshape([-1 if axis == axis_at else 1 for axis in range(len(dims))])
    return factor_of


def scatter_about(key, shape, spread, most, shards=(), kind=jnp.bfloat16):
    drawn = jax.random.normal(key, shape, jnp.float32) * spread
    if len(shards) > 0:
        drawn = level_of(key, shape, shards, -0.22, 0.18) * drawn
    return jnp.clip(drawn, min=-most, max=most).astype(kind)


def setup_inputs(seed: int = 0) -> dict:
    keys = jax.random.split(jax.random.key(seed), 8)
    vort_div = scatter_about(keys[0], (4, LEVELS, M, M), 0.05, 0.4, ((1, 4), (2, 8)), jnp.float32)
    legendre = scatter_about(keys[1], (M, LATS, M), (M // 2) ** -0.5, 1.0, ((0, 8),), jnp.float32)
    owner_map = draw_owner_map(jax.random.fold_in(keys[7], 71), 0)
    lat_sine = jnp.clip(jax.random.uniform(keys[3], (LATS,), jnp.float32, -0.9, 0.9) * level_of(keys[3], (LATS,), ((0, 8),), -0.4, 0.0), -0.9, 0.9)
    quad_weight = jnp.clip(2.0 + 4.0 * jax.random.uniform(keys[4], (LATS,), jnp.float32) ** level_of(keys[4], (LATS,), ((0, 8),), -0.2, 0.2), 2.0, 6.0)
    thickness = jnp.clip(jnp.exp(math.log(0.08) - 1.3862944 * jax.random.uniform(keys[5], (LEVELS,), jnp.float32) ** level_of(keys[5], (LEVELS,), ((0, 4),), -0.2, 0.2)), 0.02, 0.08)
    tracers = scatter_about(keys[6], (TRACERS, LEVELS, LATS, NLON), 1.0, 6.0, ((1, 4), (2, 8)), jnp.float32)
    return {"vort_div": vort_div, "legendre": legendre, "owner_map": owner_map, "lat_sine": lat_sine, "quad_weight": quad_weight, "thickness": thickness, "tracers": tracers}


planet_radius = 20.0

def spectral_winds(vort_div, wavenumbers, degrees):
    order = wavenumbers.astype(jnp.float32)[:, None]
    degree = jnp.arange(degrees).astype(jnp.float32)[None, :]
    ratio = jnp.maximum(degree * degree - order * order, 0.0) / jnp.maximum(4.0 * degree * degree - 1.0, 1.0)
    coupling = jnp.where(degree > order, jnp.sqrt(ratio), 0.0)
    inverse = jnp.where(degree > 0, -planet_radius * planet_radius / jnp.maximum(degree * (degree + 1.0), 1.0), 0.0)
    coupling_next = jnp.concatenate([coupling[:, 1:], jnp.zeros((coupling.shape[0], 1), jnp.float32)], axis=1)

    def derivative(field):
        edge = jnp.zeros(field.shape[:-1] + (1,), jnp.float32)
        lower = jnp.concatenate([edge, field[..., :-1]], axis=-1)
        upper = jnp.concatenate([field[..., 1:], edge], axis=-1)
        return -(degree - 1.0) * coupling * lower + (degree + 2.0) * coupling_next * upper
    stream_real = inverse * vort_div[0]
    stream_imag = inverse * vort_div[1]
    potential_real = inverse * vort_div[2]
    potential_imag = inverse * vort_div[3]
    east_real = (-order * potential_imag - derivative(stream_real)) / planet_radius
    east_imag = (order * potential_real - derivative(stream_imag)) / planet_radius
    north_real = (-order * stream_imag + derivative(potential_real)) / planet_radius
    north_imag = (order * stream_real + derivative(potential_imag)) / planet_radius
    return jnp.stack([east_real, east_imag, north_real, north_imag, vort_div[2], vort_div[3]], axis=0)

def reference(vort_div, legendre, owner_map, lat_sine, quad_weight, thickness, tracers):
    degrees = legendre.shape[2]
    order = owner_map.astype(jnp.float32)[:, None]
    degree = jnp.arange(degrees).astype(jnp.float32)[None, :]
    valid = degree >= order
    table = jnp.where(valid[:, None, :], legendre, 0.0)
    coefficients = spectral_winds(vort_div, owner_map, degrees)
    fourier = jnp.einsum('sjn,fksn->fkjs', table, coefficients, precision=lax.Precision.HIGHEST)
    real_part = fourier[0::2]
    imag_part = fourier[1::2]
    spread_real = jnp.zeros(real_part.shape, jnp.float32).at[..., owner_map].set(real_part)
    spread_imag = jnp.zeros(imag_part.shape, jnp.float32).at[..., owner_map].set(imag_part)
    first = jnp.arange(M) == 0
    half_real = jnp.where(first, spread_real, 0.5 * spread_real)
    half_imag = jnp.where(first, 0.0, 0.5 * spread_imag)
    spectrum = lax.complex(half_real, half_imag)
    spectrum = jnp.concatenate([spectrum, jnp.zeros(spectrum.shape[:-1] + (1,), spectrum.dtype)], axis=-1)
    grid_fields = NLON * jnp.fft.irfft(spectrum, n=NLON, axis=-1)
    east = grid_fields[0]
    north = grid_fields[1]
    divergence = grid_fields[2]
    layer_mass = divergence * thickness[:, None, None]
    column = jnp.cumsum(layer_mass, axis=0)
    omega_bottom = -column
    omega_top = layer_mass - column
    zero_level = jnp.zeros(tracers[:, :1].shape, jnp.float32)
    above = jnp.concatenate([zero_level, tracers[:, :-1]], axis=1)
    below = jnp.concatenate([tracers[:, 1:], zero_level], axis=1)
    vertical = (omega_bottom * (tracers + below) * 0.5 - omega_top * (above + tracers) * 0.5) / thickness[:, None, None]
    lon_step = 2.0 * math.pi / NLON
    lat_step = math.pi / M
    zonal_flux = east * tracers
    zonal = (jnp.roll(zonal_flux, -1, axis=3) - jnp.roll(zonal_flux, 1, axis=3)) / (2.0 * lon_step)
    merid_flux = north * tracers
    zero_row = jnp.zeros(merid_flux[:, :, :1].shape, jnp.float32)
    north_row = jnp.concatenate([merid_flux[:, :, 1:], zero_row], axis=2)
    south_row = jnp.concatenate([zero_row, merid_flux[:, :, :-1]], axis=2)
    merid = (north_row - south_row) / (2.0 * lat_step)
    metric = (1.0 - lat_sine * lat_sine)[None, None, :, None]
    grid_tendency = -quad_weight[None, None, :, None] * ((zonal + merid) / metric + vertical)
    transform = jnp.fft.rfft(grid_tendency, axis=-1)[..., :M]
    scale = 2.0 / NLON
    cos_part = scale * jnp.real(transform)
    sin_part = scale * jnp.imag(transform)
    stacked = jnp.stack([cos_part[..., owner_map], sin_part[..., owner_map]], axis=1)
    return jnp.einsum('sjn,crkjs->crksn', table, stacked, precision=lax.Precision.HIGHEST)
```

```python
import functools
import math

import jax
import jax.numpy as jnp
from jax import lax
from jax.experimental import pallas as pl
from jax.experimental.pallas import tpu as pltpu
from jax.sharding import PartitionSpec as P

planet_radius = 20.0
MESH = pl.DeviceIdType.MESH
HIGHEST = lax.Precision.HIGHEST


def up_to(size, unit):
    return -(-size // unit) * unit


def each(count, body):
    if count <= 16:
        for i in range(count):
            body(i)
    else:

        def step(i, carry):
            body(i)
            return carry

        lax.fori_loop(0, count, step, 0)


def small_sin(x):
    y = x * x
    total = jnp.full_like(y, 1.0 / 6227020800.0)
    for c in (-1.0 / 39916800.0, 1.0 / 362880.0, -1.0 / 5040.0, 1.0 / 120.0, -1.0 / 6.0, 1.0):
        total = total * y + c
    return total * x


def kernel(
    n, levels, sizes,
    vd_ref, leg_ref, owner, sine_ref, weight_ref, thick_ref, q_ref,
    out_ref,
    vdp, table, legm, msg, recv1, qs, qn, lsend, recvl, send2, recv2,
    ss1, rs1, ssq, rsq, ssl, rsl, ss2, rs2,
):
    slots, lat, degrees, length, tracers = sizes
    wl = table.shape[1] // 2
    nd = vdp.shape[2]
    sp = vdp.shape[1]
    me = lax.axis_index("wave")
    lev = lax.axis_index("lev")

    qs[...] = q_ref[:, 0, 0, :]
    qn[...] = jnp.zeros_like(qn)
    recvl[...] = jnp.zeros_like(recvl)

    barrier = pltpu.get_barrier_semaphore()

    def greet_wave(d):
        pl.semaphore_signal(
            barrier, inc=1, device_id={"wave": lax.rem(me + d + 1, n)}, device_id_type=MESH
        )

    def greet_lev(d):
        pl.semaphore_signal(
            barrier, inc=1, device_id={"lev": lax.rem(lev + d + 1, levels)}, device_id_type=MESH
        )

    each(n - 1, greet_wave)
    each(levels - 1, greet_lev)

    vdp[...] = jnp.zeros_like(vdp)
    for f in range(4):
        vdp[f, :slots, :degrees] = vd_ref[f, 0]
    orders = [owner[me * slots + s].astype(jnp.float32) for s in range(slots)]
    sub = lax.broadcasted_iota(jnp.int32, (sp, nd), 0)
    degree = lax.broadcasted_iota(jnp.int32, (sp, nd), 1).astype(jnp.float32)
    order = jnp.zeros((sp, nd), jnp.float32)
    for s in range(slots):
        order = jnp.where(sub == s, orders[s], order)

    def coupling_at(d):
        ratio = jnp.maximum(d * d - order * order, 0.0) / jnp.maximum(4.0 * d * d - 1.0, 1.0)
        return jnp.where((d > order) & (d < degrees), jnp.sqrt(ratio), 0.0)

    lower_factor = -(degree - 1.0) * coupling_at(degree)
    upper_factor = (degree + 2.0) * coupling_at(degree + 1.0)
    inverse = jnp.where(
        degree > 0, -planet_radius * planet_radius / jnp.maximum(degree * (degree + 1.0), 1.0), 0.0
    )

    def derivative(field):
        return lower_factor * pltpu.roll(field, 1, 1) + upper_factor * pltpu.roll(field, nd - 1, 1)

    stream_real = inverse * vdp[0]
    stream_imag = inverse * vdp[1]
    potential_real = inverse * vdp[2]
    potential_imag = inverse * vdp[3]
    scale = 1.0 / planet_radius
    valid = degree >= order
    coefficients = [
        jnp.where(valid, c, 0.0)
        for c in (
            (-order * potential_imag - derivative(stream_real)) * scale,
            (order * potential_real - derivative(stream_imag)) * scale,
            (-order * stream_imag + derivative(potential_real)) * scale,
            (order * stream_real + derivative(potential_imag)) * scale,
            vdp[2],
            vdp[3],
        )
    ]

    lane = lax.broadcasted_iota(jnp.int32, (lat, wl), 1)
    fourier = [jnp.zeros((lat, wl), jnp.float32) for _ in range(6)]
    for s in range(slots):
        p_s = leg_ref[s]
        here = lane == s * n + me
        for f in range(6):
            total = jnp.sum(p_s * coefficients[f][s : s + 1, :degrees], axis=1, keepdims=True)
            fourier[f] = jnp.where(here, total, fourier[f])
    row = lax.broadcasted_iota(jnp.int32, (lat, wl), 0)

    def row_before(x):
        return jnp.where(row == 0, 0.0, pltpu.roll(x, 1, 0))

    def row_after(x):
        return jnp.where(row == lat - 1, 0.0, pltpu.roll(x, lat - 1, 0))

    for part in range(2):
        east, north, div = fourier[part], fourier[2 + part], fourier[4 + part]
        for t, value in enumerate((east, row_before(north), row_after(north), div)):
            msg[:, 4 * part + t, :] = value

    pl.semaphore_wait(barrier, n + levels - 2)

    def wave_copy(source, target, send, recv, d, buffer_at, out_at):
        return pltpu.make_async_remote_copy(
            src_ref=source.at[buffer_at],
            dst_ref=target.at[out_at],
            send_sem=send.at[d],
            recv_sem=recv.at[d],
            device_id={"wave": lax.rem(me + d + 1, n)},
            device_id_type=MESH,
        )

    def first(d):
        return wave_copy(msg, recv1, ss1, rs1, d, lax.rem(me + d + 1, n), me)

    each(n - 1, lambda d: first(d).start())

    halos = (
        ("wave", me, n, 1, 0),
        ("wave", me, n, -1, 1),
        ("lev", lev, levels, 1, 2),
        ("lev", lev, levels, -1, 3),
    )

    def halo_copy(axis, place, step, k):
        return pltpu.make_async_remote_copy(
            src_ref=qs,
            dst_ref=qn.at[k],
            send_sem=ssq.at[k],
            recv_sem=rsq.at[k],
            device_id={axis: place + step},
            device_id_type=MESH,
        )

    def sends(place, count, step):
        return place < count - 1 if step > 0 else place > 0

    for axis, place, count, step, k in halos:

        @pl.when(sends(place, count, step))
        def _():
            halo_copy(axis, place, step, k).start()

    lane1 = lax.broadcasted_iota(jnp.int32, (1, wl), 1)

    def put(l, held):
        number = owner[lax.rem(l, n) * slots + l // n].astype(jnp.float32)
        return jnp.where(lane1 == l, number, held)

    numbers = jnp.zeros((1, wl), jnp.float32)
    if slots * n <= 128:
        for l in range(slots * n):
            numbers = put(l, numbers)
    else:
        numbers = lax.fori_loop(0, slots * n, put, numbers)
    filled = lane1 < slots * n
    block = 32 if length % 32 == 0 else 8 if length % 8 == 0 else length

    def table_block(b):
        start = b * block
        if not isinstance(b, int):
            start = pl.multiple_of(start, block)
        lon = lax.broadcasted_iota(jnp.int32, (block, wl), 0).astype(jnp.float32)
        if isinstance(b, int):
            lon = lon + float(start)
        else:
            lon = lon + start.astype(jnp.float32)
        product = numbers * lon
        turn = product - length * jnp.floor(product * (1.0 / length))
        turn = jnp.where(turn < 0, turn + length, turn)
        turn = jnp.where(turn >= length, turn - length, turn)
        turn = jnp.where(turn > length / 2, turn - length, turn)
        size = jnp.abs(turn)
        unit = 2.0 * math.pi / length
        cosine = small_sin((length / 4 - size) * unit)
        sine = small_sin(jnp.minimum(size, length / 2 - size) * unit)
        minus_sine = jnp.where(turn > 0, -sine, sine)
        table[pl.ds(start, block), :wl] = jnp.where(filled, cosine, 0.0)
        table[pl.ds(start, block), wl:] = jnp.where(filled, minus_sine, 0.0)

    each(length // block, table_block)
    degree_row = lax.broadcasted_iota(jnp.int32, (lat, degrees), 1).astype(jnp.float32)
    for s in range(slots):
        legm[pl.ds(s * lat, lat), :] = jnp.where(degree_row >= orders[s], leg_ref[s], 0.0)

    recv1[me] = msg[me]

    def first_wait(d):
        source = lax.rem(me - d - 1 + n, n)
        pltpu.make_async_remote_copy(
            src_ref=msg.at[0],
            dst_ref=recv1.at[source],
            send_sem=ss1.at[d],
            recv_sem=rs1.at[d],
            device_id={"wave": source},
            device_id_type=MESH,
        ).wait_recv()

    each(n - 1, first_wait)
    got = jnp.sum(recv1[...], axis=0)
    thick = jnp.full((1, 1), thick_ref[0], jnp.float32)

    lsend[...] = got * thick

    def level_copy(d):
        return pltpu.make_async_remote_copy(
            src_ref=lsend,
            dst_ref=recvl.at[lev],
            send_sem=ssl.at[d],
            recv_sem=rsl.at[d],
            device_id={"lev": lev + d + 1},
            device_id_type=MESH,
        )

    def level_start(d):
        @pl.when(lev + d + 1 < levels)
        def _():
            level_copy(d).start()

    each(levels - 1, level_start)

    def to_grid(left):
        return lax.dot_general(
            left, table[...], (((1,), (1,)), ((), ())),
            precision=HIGHEST, preferred_element_type=jnp.float32,
        )

    grid = to_grid(jnp.concatenate([got[0:4], got[4:8]], axis=1))
    q = qs[...]
    lon_step = 2.0 * math.pi / length
    lat_step = math.pi / (slots * n)
    flux = grid[0:1] * q
    ahead = jnp.concatenate([flux[:, 1:], flux[:, :1]], axis=1)
    behind = jnp.concatenate([flux[:, -1:], flux[:, :-1]], axis=1)
    zonal = (ahead - behind) * (1.0 / (2.0 * lon_step))

    for axis, place, count, step, k in halos:

        @pl.when(sends(place, count, -step))
        def _():
            halo_copy(axis, place, -step, k).wait_recv()

    merid = (grid[2:3] * qn[1] - grid[1:2] * qn[0]) * (1.0 / (2.0 * lat_step))
    sine = jnp.full((1, 1), sine_ref[0], jnp.float32)
    base = (zonal + merid) / (1.0 - sine * sine)
    layer = grid[3:4] * thick
    above = qn[2]
    below = qn[3]

    def level_wait(d):
        @pl.when(lev - d - 1 >= 0)
        def _():
            pltpu.make_async_remote_copy(
                src_ref=lsend,
                dst_ref=recvl.at[lev - d - 1],
                send_sem=ssl.at[d],
                recv_sem=rsl.at[d],
                device_id={"lev": lev - d - 1},
                device_id_type=MESH,
            ).wait_recv()

    each(levels - 1, level_wait)
    higher = jnp.sum(recvl[...], axis=0)
    prefix = to_grid(jnp.concatenate([higher[3:4], higher[7:8]], axis=1))
    omega_bottom = -(prefix + layer)
    omega_top = -prefix
    vertical = (omega_bottom * (q + below) * 0.5 - omega_top * (above + q) * 0.5) / thick
    weight = jnp.full((1, 1), weight_ref[0], jnp.float32)
    tendency = -weight * (base + vertical)

    spectra = lax.dot_general(
        tendency, table[...], (((1,), (0,)), ((), ())),
        precision=HIGHEST, preferred_element_type=jnp.float32,
    ) * (2.0 / length)
    spectra = jnp.concatenate([spectra[:, :wl], spectra[:, wl:]], axis=0)

    def second(d):
        return wave_copy(send2, recv2, ss2, rs2, d, d, me)

    def second_start(d):
        shift = lax.rem(wl + me - lax.rem(me + d + 1, n), wl)
        send2[d] = pltpu.roll(spectra, shift, 1)
        second(d).start()

    each(n - 1, second_start)
    recv2[me] = spectra

    def second_wait(d):
        source = lax.rem(me - d - 1 + n, n)
        pltpu.make_async_remote_copy(
            src_ref=send2.at[d],
            dst_ref=recv2.at[source],
            send_sem=ss2.at[d],
            recv_sem=rs2.at[d],
            device_id={"wave": source},
            device_id_type=MESH,
        ).wait_recv()

    each(n - 1, second_wait)
    lane2 = lax.broadcasted_iota(jnp.int32, (2 * tracers, wl), 1)
    row_of = lax.rem(lane2, n)
    gathered = jnp.zeros((2 * tracers, wl), jnp.float32)
    if n <= 16:
        for i in range(n):
            gathered = jnp.where(row_of == i, recv2[i], gathered)
    else:
        gathered = lax.fori_loop(
            0, n, lambda i, g: jnp.where(row_of == i, recv2[i], g), gathered
        )
    lane3 = lax.broadcasted_iota(jnp.int32, (sp, wl), 1)
    sub3 = lax.broadcasted_iota(jnp.int32, (sp, wl), 0)
    own = (lane3 >= sub3 * n) & (lane3 < sub3 * n + n)
    blocks = []
    for c in range(tracers):
        for r in range(2):
            i = r * tracers + c
            blocks.append(jnp.where(own, gathered[i : i + 1], 0.0))
    left = jnp.concatenate(blocks, axis=0)[:, : slots * n]
    result = jnp.dot(left, legm[...], precision=HIGHEST, preferred_element_type=jnp.float32)
    for c in range(tracers):
        for r in range(2):
            at = (c * 2 + r) * sp
            out_ref[c, r, 0] = result[at : at + slots]

    each(n - 1, lambda d: first(d).wait_send())
    each(n - 1, lambda d: second(d).wait_send())
    for axis, place, count, step, k in halos:

        @pl.when(sends(place, count, step))
        def _():
            halo_copy(axis, place, step, k).wait_send()

    def level_sent(d):
        @pl.when(lev + d + 1 < levels)
        def _():
            level_copy(d).wait_send()

    each(levels - 1, level_sent)


def shards(vort_div, legendre, owner_map, lat_sine, quad_weight, thickness, tracers):
    slots, lat, degrees = legendre.shape
    count, own_levels, own_rows, length = tracers.shape
    n, levels = lax.axis_size("wave"), lax.axis_size("lev")
    assert own_levels == 1 and own_rows == 1 and lat == n
    wl = up_to(slots * n, 128)
    nd = up_to(degrees, 128)
    sp = up_to(slots, 8)
    f32 = jnp.float32
    shapes = [
        ((4, sp, nd), f32),
        ((length, 2 * wl), f32),
        ((slots * lat, degrees), f32),
        ((n, 8, wl), f32),
        ((n, 8, wl), f32),
        ((count, length), f32),
        ((4, count, length), f32),
        ((8, wl), f32),
        ((levels, 8, wl), f32),
        ((n - 1, 2 * count, wl), f32),
        ((n, 2 * count, wl), f32),
    ]
    dma = pltpu.SemaphoreType.DMA
    vmem = pl.BlockSpec(memory_space=pltpu.VMEM)
    smem = pl.BlockSpec(memory_space=pltpu.SMEM)
    scratch_bytes = sum(4 * math.prod(shape) for shape, _ in shapes)
    return pl.pallas_call(
        functools.partial(kernel, n, levels, (slots, lat, degrees, length, count)),
        out_shape=jax.ShapeDtypeStruct((count, 2, 1, slots, degrees), f32),
        in_specs=[vmem, vmem, smem, smem, smem, smem, vmem],
        out_specs=vmem,
        scratch_shapes=[pltpu.VMEM(shape, kind) for shape, kind in shapes]
        + [dma((n - 1,)), dma((n - 1,)), dma((4,)), dma((4,))]
        + [dma((levels - 1,)), dma((levels - 1,)), dma((n - 1,)), dma((n - 1,))],
        compiler_params=pltpu.CompilerParams(
            collective_id=0,
            has_side_effects=True,
            vmem_limit_bytes=min(2 * scratch_bytes + (12 << 20), 60 << 20),
        ),
    )(vort_div, legendre, owner_map, lat_sine, quad_weight, thickness, tracers)


def solution(mesh):
    placed = (
        P(None, "lev", "wave", None),
        P("wave", None, None),
        P(),
        P("wave"),
        P("wave"),
        P("lev"),
        P(None, "lev", "wave", None),
    )
    return jax.shard_map(
        shards,
        mesh=mesh,
        in_specs=placed,
        out_specs=P(None, None, "lev", "wave", None),
        check_vma=False,
    )
```

```python
import functools
import math

import jax
import jax.numpy as jnp
from jax import lax
from jax.experimental import pallas as pl
from jax.experimental.pallas import tpu as pltpu
from jax.sharding import PartitionSpec as P

planet_radius = 20.0
MESH = pl.DeviceIdType.MESH


def up_to(size, unit):
    return -(-size // unit) * unit


def each(count, body):
    if count <= 32:
        for i in range(count):
            body(i)
    else:

        def step(i, carry):
            body(i)
            return carry

        lax.fori_loop(0, count, step, 0)


def halves(x):
    high = x.astype(jnp.bfloat16).astype(jnp.float32)
    return high, x - high


def split_dot(left, right_high, right_low, dims):
    rows = left.shape[0]
    high, low = halves(left)
    both = jnp.concatenate([high, low], axis=0).astype(jnp.bfloat16)
    dot = functools.partial(
        lax.dot_general, dimension_numbers=(dims, ((), ())), preferred_element_type=jnp.float32
    )
    first = dot(both, right_high)
    return first[:rows] + first[rows:] + dot(high.astype(jnp.bfloat16), right_low)


def small_sin(x):
    y = x * x
    total = jnp.full_like(y, 1.0 / 6227020800.0)
    for c in (-1.0 / 39916800.0, 1.0 / 362880.0, -1.0 / 5040.0, 1.0 / 120.0, -1.0 / 6.0, 1.0):
        total = total * y + c
    return total * x


def kernel(
    n, levels, sizes,
    vd_in, leg_in, owner_in, sine_in, weight_in, thick_in, q_in,
    out_ref,
    vd_ref, leg_ref, owner_ref, sine_ref, weight_ref, thick_ref, q_ref,
    vdp, thigh, tlow, lhigh, llow, msg, recv1, qs, qn, dmsg, recvd, send2, recv2,
    ssi, ss1, rs1, ssq, rsq, ssd, rsd, ss2, rs2,
):
    slots, lat, degrees, length, tracers = sizes
    wl = thigh.shape[1] // 2
    nd = vdp.shape[2]
    sp = vdp.shape[1]
    me = lax.axis_index("wave")
    lev = lax.axis_index("lev")

    loads = [
        pltpu.make_async_copy(source, target, ssi.at[i])
        for i, (source, target) in enumerate(
            (
                (vd_in, vd_ref),
                (owner_in, owner_ref),
                (leg_in, leg_ref),
                (q_in, q_ref),
                (thick_in, thick_ref),
                (sine_in, sine_ref),
                (weight_in, weight_ref),
            )
        )
    ]
    for load in loads:
        load.start()
    qn[...] = jnp.zeros_like(qn)
    recvd[...] = jnp.zeros_like(recvd)

    barrier = pltpu.get_barrier_semaphore()

    def greet(d):
        pl.semaphore_signal(
            barrier,
            inc=1,
            device_id={
                "wave": lax.rem(me + (d + 1) % n, n),
                "lev": lax.rem(lev + (d + 1) // n, levels),
            },
            device_id_type=MESH,
        )

    each(n * levels - 1, greet)

    vdp[...] = jnp.zeros_like(vdp)
    for load in loads:
        load.wait()
    for f in range(4):
        vdp[f, :slots, :degrees] = vd_ref[f, :, 0]
    qs[...] = q_ref[:, 0, 0, :]
    owner = owner_ref[...].astype(jnp.float32)
    total_slots = owner.shape[1]
    place_at = lax.broadcasted_iota(jnp.int32, (sp, total_slots), 1)
    slot_at = lax.broadcasted_iota(jnp.int32, (sp, total_slots), 0)
    own_order = jnp.sum(
        jnp.where(place_at == me * slots + slot_at, owner, 0.0), axis=1, keepdims=True
    )
    thick = thick_ref[...].reshape(1, 1)
    sub = lax.broadcasted_iota(jnp.int32, (sp, nd), 0)
    degree = lax.broadcasted_iota(jnp.int32, (sp, nd), 1).astype(jnp.float32)
    order = jnp.where(sub < slots, own_order, 0.0)

    def coupling_at(d):
        ratio = jnp.maximum(d * d - order * order, 0.0) / jnp.maximum(4.0 * d * d - 1.0, 1.0)
        return jnp.where((d > order) & (d < degrees), jnp.sqrt(ratio), 0.0)

    lower_factor = -(degree - 1.0) * coupling_at(degree)
    upper_factor = (degree + 2.0) * coupling_at(degree + 1.0)
    inverse = jnp.where(
        degree > 0, -planet_radius * planet_radius / jnp.maximum(degree * (degree + 1.0), 1.0), 0.0
    )

    def derivative(field):
        return lower_factor * pltpu.roll(field, 1, 1) + upper_factor * pltpu.roll(field, nd - 1, 1)

    stream_real = inverse * vdp[0]
    stream_imag = inverse * vdp[1]
    potential_real = inverse * vdp[2]
    potential_imag = inverse * vdp[3]
    scale = 1.0 / planet_radius
    valid = degree >= order
    coefficients = [
        jnp.where(valid, c, 0.0)
        for c in (
            (-order * potential_imag - derivative(stream_real)) * scale,
            (order * potential_real - derivative(stream_imag)) * scale,
            (-order * stream_imag + derivative(potential_real)) * scale,
            (order * stream_real + derivative(potential_imag)) * scale,
            vdp[2],
            vdp[3],
        )
    ]

    lane = lax.broadcasted_iota(jnp.int32, (lat, wl), 1)
    fourier = [jnp.zeros((lat, wl), jnp.float32) for _ in range(6)]
    for s in range(slots):
        p_s = leg_ref[s]
        here = lane == s * n + me
        for f in range(6):
            total = jnp.sum(p_s * coefficients[f][s : s + 1, :degrees], axis=1, keepdims=True)
            fourier[f] = jnp.where(here, total, fourier[f])
    row = lax.broadcasted_iota(jnp.int32, (lat, wl), 0)

    def row_before(x):
        return jnp.where(row == 0, 0.0, pltpu.roll(x, 1, 0))

    def row_after(x):
        return jnp.where(row == lat - 1, 0.0, pltpu.roll(x, lat - 1, 0))

    for part in range(2):
        east, north, div = fourier[part], fourier[2 + part], fourier[4 + part]
        for t, value in enumerate((east, row_before(north), row_after(north), div)):
            msg[:, 4 * part + t, :] = value
        dmsg[:, part, :] = div * thick

    pl.semaphore_wait(barrier, n * levels - 1)

    def wave_copy(source, target, send, recv, d, buffer_at, out_at):
        return pltpu.make_async_remote_copy(
            src_ref=source.at[buffer_at],
            dst_ref=target.at[out_at],
            send_sem=send.at[d],
            recv_sem=recv.at[d],
            device_id={"wave": lax.rem(me + d + 1, n)},
            device_id_type=MESH,
        )

    def first(d):
        return wave_copy(msg, recv1, ss1, rs1, d, lax.rem(me + d + 1, n), me)

    each(n - 1, lambda d: first(d).start())

    def mass(k):
        up, to = k // n, k % n

        @pl.when(lev + up + 1 < levels)
        def _():
            pltpu.make_async_remote_copy(
                src_ref=dmsg.at[to],
                dst_ref=recvd.at[lev, me],
                send_sem=ssd.at[up],
                recv_sem=rsd.at[up],
                device_id={"wave": to, "lev": lev + up + 1},
                device_id_type=MESH,
            ).start()

    each((levels - 1) * n, mass)

    halos = (
        ("wave", me, n, 1, 0),
        ("wave", me, n, -1, 1),
        ("lev", lev, levels, 1, 2),
        ("lev", lev, levels, -1, 3),
    )

    def halo_copy(axis, place, step, k):
        return pltpu.make_async_remote_copy(
            src_ref=qs,
            dst_ref=qn.at[k],
            send_sem=ssq.at[k],
            recv_sem=rsq.at[k],
            device_id={axis: place + step},
            device_id_type=MESH,
        )

    def sends(place, count, step):
        return place < count - 1 if step > 0 else place > 0

    for axis, place, count, step, k in halos:

        @pl.when(sends(place, count, step))
        def _():
            halo_copy(axis, place, step, k).start()

    lane1 = lax.broadcasted_iota(jnp.int32, (1, wl), 1)
    target = lax.broadcasted_iota(jnp.int32, (wl, total_slots), 0)
    source_at = lax.broadcasted_iota(jnp.int32, (wl, total_slots), 1)
    column = jnp.sum(
        jnp.where(source_at == lax.rem(target, n) * slots + target // n, owner, 0.0),
        axis=1,
        keepdims=True,
    )
    square = (wl, wl)
    diagonal = lax.broadcasted_iota(jnp.int32, square, 0) == lax.broadcasted_iota(jnp.int32, square, 1)
    numbers = jnp.sum(jnp.where(diagonal, column, 0.0), axis=0, keepdims=True)
    filled = lane1 < slots * n
    block = 32 if length % 32 == 0 else 8 if length % 8 == 0 else length

    def table_block(b):
        start = b * block
        if not isinstance(b, int):
            start = pl.multiple_of(start, block)
        lon = lax.broadcasted_iota(jnp.int32, (block, wl), 0).astype(jnp.float32)
        if isinstance(b, int):
            lon = lon + float(start)
        else:
            lon = lon + start.astype(jnp.float32)
        product = numbers * lon
        turn = product - length * jnp.floor(product * (1.0 / length))
        turn = jnp.where(turn < 0, turn + length, turn)
        turn = jnp.where(turn >= length, turn - length, turn)
        turn = jnp.where(turn > length / 2, turn - length, turn)
        size = jnp.abs(turn)
        unit = 2.0 * math.pi / length
        cosine = small_sin((length / 4 - size) * unit)
        sine = small_sin(jnp.minimum(size, length / 2 - size) * unit)
        minus_sine = jnp.where(turn > 0, -sine, sine)
        for part, value in enumerate((cosine, minus_sine)):
            high, low = halves(jnp.where(filled, value, 0.0))
            at = (pl.ds(start, block), pl.ds(part * wl, wl))
            thigh[at] = high.astype(jnp.bfloat16)
            tlow[at] = low.astype(jnp.bfloat16)

    each(length // block, table_block)
    degree_row = lax.broadcasted_iota(jnp.int32, (lat, degrees), 1).astype(jnp.float32)
    masked = jnp.concatenate(
        [jnp.where(degree_row >= own_order[s : s + 1], leg_ref[s], 0.0) for s in range(slots)], axis=0
    )
    high, low = halves(masked)
    lhigh[...] = high.astype(jnp.bfloat16)
    llow[...] = low.astype(jnp.bfloat16)

    recv1[me] = msg[me]

    def first_wait(d):
        source = lax.rem(me - d - 1 + n, n)
        pltpu.make_async_remote_copy(
            src_ref=msg.at[0],
            dst_ref=recv1.at[source],
            send_sem=ss1.at[d],
            recv_sem=rs1.at[d],
            device_id={"wave": source},
            device_id_type=MESH,
        ).wait_recv()

    each(n - 1, first_wait)
    got = jnp.sum(recv1[...], axis=0)

    def mass_wait(d):
        @pl.when(lev - d - 1 >= 0)
        def _():
            pltpu.make_async_remote_copy(
                src_ref=dmsg,
                dst_ref=recvd.at[lev - d - 1],
                send_sem=ssd.at[d],
                recv_sem=rsd.at[d],
                device_id={"lev": lev - d - 1},
                device_id_type=MESH,
            ).wait_recv()

    each(levels - 1, mass_wait)
    higher = jnp.sum(jnp.sum(recvd[...], axis=0), axis=0)
    left = jnp.concatenate(
        [
            jnp.concatenate([got[0:4], higher[0:1], jnp.zeros((3, wl), jnp.float32)], axis=0),
            jnp.concatenate([got[4:8], higher[1:2], jnp.zeros((3, wl), jnp.float32)], axis=0),
        ],
        axis=1,
    )
    grid = split_dot(left, thigh[...], tlow[...], ((1,), (1,)))
    q = qs[...]
    lon_step = 2.0 * math.pi / length
    lat_step = math.pi / (slots * n)
    flux = grid[0:1] * q
    ahead = jnp.concatenate([flux[:, 1:], flux[:, :1]], axis=1)
    behind = jnp.concatenate([flux[:, -1:], flux[:, :-1]], axis=1)
    zonal = (ahead - behind) * (1.0 / (2.0 * lon_step))

    for axis, place, count, step, k in halos:

        @pl.when(sends(place, count, -step))
        def _():
            halo_copy(axis, place, -step, k).wait_recv()

    merid = (grid[2:3] * qn[1] - grid[1:2] * qn[0]) * (1.0 / (2.0 * lat_step))
    sine = sine_ref[...].reshape(1, 1)
    base = (zonal + merid) / (1.0 - sine * sine)
    layer = grid[3:4] * thick
    above = qn[2]
    below = qn[3]

    prefix = grid[4:5]
    omega_bottom = -(prefix + layer)
    omega_top = -prefix
    vertical = (omega_bottom * (q + below) * 0.5 - omega_top * (above + q) * 0.5) / thick
    tendency = -weight_ref[...].reshape(1, 1) * (base + vertical)

    spectra = split_dot(tendency, thigh[...], tlow[...], ((1,), (0,))) * (2.0 / length)
    spectra = jnp.concatenate([spectra[:, :wl], spectra[:, wl:]], axis=0)

    def second(d):
        return wave_copy(send2, recv2, ss2, rs2, d, d, me)

    def second_start(d):
        shift = lax.rem(wl + me - lax.rem(me + d + 1, n), wl)
        send2[d] = pltpu.roll(spectra, shift, 1)
        second(d).start()

    each(n - 1, second_start)
    recv2[me] = spectra

    def second_wait(d):
        source = lax.rem(me - d - 1 + n, n)
        pltpu.make_async_remote_copy(
            src_ref=send2.at[d],
            dst_ref=recv2.at[source],
            send_sem=ss2.at[d],
            recv_sem=rs2.at[d],
            device_id={"wave": source},
            device_id_type=MESH,
        ).wait_recv()

    each(n - 1, second_wait)
    lane2 = lax.broadcasted_iota(jnp.int32, (2 * tracers, wl), 1)
    row_of = lax.rem(lane2, n)
    gathered = jnp.zeros((2 * tracers, wl), jnp.float32)
    if n <= 16:
        for i in range(n):
            gathered = jnp.where(row_of == i, recv2[i], gathered)
    else:
        gathered = lax.fori_loop(
            0, n, lambda i, g: jnp.where(row_of == i, recv2[i], g), gathered
        )
    lane3 = lax.broadcasted_iota(jnp.int32, (sp, wl), 1)
    sub3 = lax.broadcasted_iota(jnp.int32, (sp, wl), 0)
    own = (lane3 >= sub3 * n) & (lane3 < sub3 * n + n)
    blocks = []
    for c in range(tracers):
        for r in range(2):
            i = r * tracers + c
            blocks.append(jnp.where(own, gathered[i : i + 1], 0.0))
    left = jnp.concatenate(blocks, axis=0)[:, : slots * n]
    result = split_dot(left, lhigh[...], llow[...], ((1,), (0,)))
    for c in range(tracers):
        for r in range(2):
            at = (c * 2 + r) * sp
            out_ref[c, r, :, 0, :] = result[at : at + slots]

    each(n - 1, lambda d: first(d).wait_send())
    each(n - 1, lambda d: second(d).wait_send())
    for axis, place, count, step, k in halos:

        @pl.when(sends(place, count, step))
        def _():
            halo_copy(axis, place, step, k).wait_send()

    def mass_sent(d):
        @pl.when(lev + d + 1 < levels)
        def _():
            pltpu.make_async_remote_copy(
                src_ref=dmsg,
                dst_ref=recvd.at[lev],
                send_sem=ssd.at[d],
                recv_sem=rsd.at[d],
                device_id={"lev": lev + d + 1},
                device_id_type=MESH,
            ).wait_send()

    each(levels - 1, mass_sent)


def shards(vort_div, legendre, owner_map, lat_sine, quad_weight, thickness, tracers):
    slots, lat, degrees = legendre.shape
    count, own_levels, own_rows, length = tracers.shape
    n, levels = lax.axis_size("wave"), lax.axis_size("lev")
    assert own_levels == 1 and own_rows == 1 and lat == n
    wl = up_to(slots * n, 128)
    nd = up_to(degrees, 128)
    sp = up_to(slots, 8)
    f32 = jnp.float32
    bf16 = jnp.bfloat16
    operands = (
        jnp.transpose(vort_div, (0, 2, 1, 3)),
        legendre,
        owner_map.reshape(1, -1),
        lat_sine,
        quad_weight,
        thickness,
        tracers,
    )
    shapes = [(x.shape, x.dtype) for x in operands] + [
        ((4, sp, nd), f32),
        ((length, 2 * wl), bf16),
        ((length, 2 * wl), bf16),
        ((slots * lat, degrees), bf16),
        ((slots * lat, degrees), bf16),
        ((n, 8, wl), f32),
        ((n, 8, wl), f32),
        ((count, length), f32),
        ((4, count, length), f32),
        ((n, 2, wl), f32),
        ((levels, n, 2, wl), f32),
        ((n - 1, 2 * count, wl), f32),
        ((n, 2 * count, wl), f32),
    ]
    dma = pltpu.SemaphoreType.DMA
    scratch_bytes = sum(4 * math.prod(shape) for shape, _ in shapes)
    result = pl.pallas_call(
        functools.partial(kernel, n, levels, (slots, lat, degrees, length, count)),
        out_shape=jax.ShapeDtypeStruct((count, 2, slots, 1, degrees), f32),
        in_specs=[pl.BlockSpec(memory_space=pltpu.HBM)] * len(operands),
        out_specs=pl.BlockSpec(memory_space=pltpu.VMEM),
        scratch_shapes=[pltpu.VMEM(shape, kind) for shape, kind in shapes]
        + [dma((len(operands),)), dma((n - 1,)), dma((n - 1,)), dma((4,)), dma((4,))]
        + [dma((levels - 1,)), dma((levels - 1,)), dma((n - 1,)), dma((n - 1,))],
        compiler_params=pltpu.CompilerParams(
            collective_id=0,
            has_side_effects=True,
            vmem_limit_bytes=63 << 20,
        ),
    )(*operands)
    return jnp.transpose(result, (0, 1, 3, 2, 4))


def solution(mesh):
    placed = (
        P(None, "lev", "wave", None),
        P("wave", None, None),
        P(),
        P("wave"),
        P("wave"),
        P("lev"),
        P(None, "lev", "wave", None),
    )
    return jax.shard_map(
        shards,
        mesh=mesh,
        in_specs=placed,
        out_specs=P(None, None, "lev", "wave", None),
        check_vma=False,
    )
```

```python
import functools
import math

import jax
import jax.numpy as jnp
from jax import lax
from jax.experimental import pallas as pl
from jax.experimental.pallas import tpu as pltpu
from jax.sharding import PartitionSpec as P

planet_radius = 20.0
MESH = pl.DeviceIdType.MESH


def up_to(size, unit):
    return -(-size // unit) * unit


def each(count, body):
    if count <= 32:
        for i in range(count):
            body(i)
    else:

        def step(i, carry):
            body(i)
            return carry

        lax.fori_loop(0, count, step, 0)


def halves(x):
    high = x.astype(jnp.bfloat16).astype(jnp.float32)
    return high, x - high


def split_dot(left, right_high, right_low, dims):
    rows = left.shape[0]
    high, low = halves(left)
    both = jnp.concatenate([high, low], axis=0).astype(jnp.bfloat16)
    dot = functools.partial(
        lax.dot_general, dimension_numbers=(dims, ((), ())), preferred_element_type=jnp.float32
    )
    first = dot(both, right_high)
    return first[:rows] + first[rows:] + dot(high.astype(jnp.bfloat16), right_low)


def small_sin(x):
    y = x * x
    total = jnp.full_like(y, 1.0 / 6227020800.0)
    for c in (-1.0 / 39916800.0, 1.0 / 362880.0, -1.0 / 5040.0, 1.0 / 120.0, -1.0 / 6.0, 1.0):
        total = total * y + c
    return total * x


def kernel(
    n, levels, sizes,
    vd_ref, leg_ref, owner_ref, sine_ref, weight_ref, thick_ref, q_ref,
    out_ref,
    vdp, thigh, tlow, lhigh, llow, msg, recv1, qs, qn, dmsg, recvd, send2, recv2,
    ss1, rs1, ssq, rsq, ssd, rsd, ss2, rs2,
):
    slots, lat, degrees, length, tracers = sizes
    wl = thigh.shape[1] // 2
    nd = vdp.shape[2]
    sp = vdp.shape[1]
    me = lax.axis_index("wave")
    lev = lax.axis_index("lev")

    qn[...] = jnp.zeros_like(qn)
    recvd[...] = jnp.zeros_like(recvd)

    barrier = pltpu.get_barrier_semaphore()

    def greet(d):
        pl.semaphore_signal(
            barrier,
            inc=1,
            device_id={
                "wave": lax.rem(me + (d + 1) % n, n),
                "lev": lax.rem(lev + (d + 1) // n, levels),
            },
            device_id_type=MESH,
        )

    each(n * levels - 1, greet)

    vdp[...] = jnp.zeros_like(vdp)
    for f in range(4):
        vdp[f, :slots, :degrees] = vd_ref[f, :, 0]
    qs[...] = q_ref[:, 0, 0, :]
    owner = owner_ref[...].astype(jnp.float32)
    total_slots = owner.shape[1]
    place_at = lax.broadcasted_iota(jnp.int32, (sp, total_slots), 1)
    slot_at = lax.broadcasted_iota(jnp.int32, (sp, total_slots), 0)
    own_order = jnp.sum(
        jnp.where(place_at == me * slots + slot_at, owner, 0.0), axis=1, keepdims=True
    )
    thick = thick_ref[...].reshape(1, 1)
    sub = lax.broadcasted_iota(jnp.int32, (sp, nd), 0)
    degree = lax.broadcasted_iota(jnp.int32, (sp, nd), 1).astype(jnp.float32)
    order = jnp.where(sub < slots, own_order, 0.0)

    def coupling_at(d):
        ratio = jnp.maximum(d * d - order * order, 0.0) / jnp.maximum(4.0 * d * d - 1.0, 1.0)
        return jnp.where((d > order) & (d < degrees), jnp.sqrt(ratio), 0.0)

    lower_factor = -(degree - 1.0) * coupling_at(degree)
    upper_factor = (degree + 2.0) * coupling_at(degree + 1.0)
    inverse = jnp.where(
        degree > 0, -planet_radius * planet_radius / jnp.maximum(degree * (degree + 1.0), 1.0), 0.0
    )

    def derivative(field):
        return lower_factor * pltpu.roll(field, 1, 1) + upper_factor * pltpu.roll(field, nd - 1, 1)

    stream_real = inverse * vdp[0]
    stream_imag = inverse * vdp[1]
    potential_real = inverse * vdp[2]
    potential_imag = inverse * vdp[3]
    scale = 1.0 / planet_radius
    valid = degree >= order
    coefficients = [
        jnp.where(valid, c, 0.0)
        for c in (
            (-order * potential_imag - derivative(stream_real)) * scale,
            (order * potential_real - derivative(stream_imag)) * scale,
            (-order * stream_imag + derivative(potential_real)) * scale,
            (order * stream_real + derivative(potential_imag)) * scale,
            vdp[2],
            vdp[3],
        )
    ]

    lane = lax.broadcasted_iota(jnp.int32, (lat, wl), 1)
    fourier = [jnp.zeros((lat, wl), jnp.float32) for _ in range(6)]
    for s in range(slots):
        p_s = leg_ref[s]
        here = lane == s * n + me
        for f in range(6):
            total = jnp.sum(p_s * coefficients[f][s : s + 1, :degrees], axis=1, keepdims=True)
            fourier[f] = jnp.where(here, total, fourier[f])
    row = lax.broadcasted_iota(jnp.int32, (lat, wl), 0)

    def row_before(x):
        return jnp.where(row == 0, 0.0, pltpu.roll(x, 1, 0))

    def row_after(x):
        return jnp.where(row == lat - 1, 0.0, pltpu.roll(x, lat - 1, 0))

    for part in range(2):
        east, north, div = fourier[part], fourier[2 + part], fourier[4 + part]
        for t, value in enumerate((east, row_before(north), row_after(north), div)):
            msg[:, 4 * part + t, :] = value
        dmsg[:, part, :] = div * thick

    pl.semaphore_wait(barrier, n * levels - 1)

    def wave_copy(source, target, send, recv, d, buffer_at, out_at):
        return pltpu.make_async_remote_copy(
            src_ref=source.at[buffer_at],
            dst_ref=target.at[out_at],
            send_sem=send.at[d],
            recv_sem=recv.at[d],
            device_id={"wave": lax.rem(me + d + 1, n)},
            device_id_type=MESH,
        )

    def first(d):
        return wave_copy(msg, recv1, ss1, rs1, d, lax.rem(me + d + 1, n), me)

    each(n - 1, lambda d: first(d).start())

    def mass(k):
        up, to = k // n, k % n

        @pl.when(lev + up + 1 < levels)
        def _():
            pltpu.make_async_remote_copy(
                src_ref=dmsg.at[to],
                dst_ref=recvd.at[lev, me],
                send_sem=ssd.at[up],
                recv_sem=rsd.at[up],
                device_id={"wave": to, "lev": lev + up + 1},
                device_id_type=MESH,
            ).start()

    each((levels - 1) * n, mass)

    halos = (
        ("wave", me, n, 1, 0),
        ("wave", me, n, -1, 1),
        ("lev", lev, levels, 1, 2),
        ("lev", lev, levels, -1, 3),
    )

    def halo_copy(axis, place, step, k):
        return pltpu.make_async_remote_copy(
            src_ref=qs,
            dst_ref=qn.at[k],
            send_sem=ssq.at[k],
            recv_sem=rsq.at[k],
            device_id={axis: place + step},
            device_id_type=MESH,
        )

    def sends(place, count, step):
        return place < count - 1 if step > 0 else place > 0

    for axis, place, count, step, k in halos:

        @pl.when(sends(place, count, step))
        def _():
            halo_copy(axis, place, step, k).start()

    lane1 = lax.broadcasted_iota(jnp.int32, (1, wl), 1)
    target = lax.broadcasted_iota(jnp.int32, (wl, total_slots), 0)
    source_at = lax.broadcasted_iota(jnp.int32, (wl, total_slots), 1)
    column = jnp.sum(
        jnp.where(source_at == lax.rem(target, n) * slots + target // n, owner, 0.0),
        axis=1,
        keepdims=True,
    )
    square = (wl, wl)
    diagonal = lax.broadcasted_iota(jnp.int32, square, 0) == lax.broadcasted_iota(jnp.int32, square, 1)
    numbers = jnp.sum(jnp.where(diagonal, column, 0.0), axis=0, keepdims=True)
    filled = lane1 < slots * n
    block = 32 if length % 32 == 0 else 8 if length % 8 == 0 else length

    def table_block(b):
        start = b * block
        if not isinstance(b, int):
            start = pl.multiple_of(start, block)
        lon = lax.broadcasted_iota(jnp.int32, (block, wl), 0).astype(jnp.float32)
        if isinstance(b, int):
            lon = lon + float(start)
        else:
            lon = lon + start.astype(jnp.float32)
        product = numbers * lon
        turn = product - length * jnp.floor(product * (1.0 / length))
        turn = jnp.where(turn < 0, turn + length, turn)
        turn = jnp.where(turn >= length, turn - length, turn)
        turn = jnp.where(turn > length / 2, turn - length, turn)
        size = jnp.abs(turn)
        unit = 2.0 * math.pi / length
        cosine = small_sin((length / 4 - size) * unit)
        sine = small_sin(jnp.minimum(size, length / 2 - size) * unit)
        minus_sine = jnp.where(turn > 0, -sine, sine)
        for part, value in enumerate((cosine, minus_sine)):
            high, low = halves(jnp.where(filled, value, 0.0))
            at = (pl.ds(start, block), pl.ds(part * wl, wl))
            thigh[at] = high.astype(jnp.bfloat16)
            tlow[at] = low.astype(jnp.bfloat16)

    each(length // block, table_block)
    degree_row = lax.broadcasted_iota(jnp.int32, (lat, degrees), 1).astype(jnp.float32)
    masked = jnp.concatenate(
        [jnp.where(degree_row >= own_order[s : s + 1], leg_ref[s], 0.0) for s in range(slots)], axis=0
    )
    high, low = halves(masked)
    lhigh[...] = high.astype(jnp.bfloat16)
    llow[...] = low.astype(jnp.bfloat16)

    recv1[me] = msg[me]

    def first_wait(d):
        source = lax.rem(me - d - 1 + n, n)
        pltpu.make_async_remote_copy(
            src_ref=msg.at[0],
            dst_ref=recv1.at[source],
            send_sem=ss1.at[d],
            recv_sem=rs1.at[d],
            device_id={"wave": source},
            device_id_type=MESH,
        ).wait_recv()

    each(n - 1, first_wait)
    got = jnp.sum(recv1[...], axis=0)

    def mass_wait(d):
        @pl.when(lev - d - 1 >= 0)
        def _():
            pltpu.make_async_remote_copy(
                src_ref=dmsg,
                dst_ref=recvd.at[lev - d - 1],
                send_sem=ssd.at[d],
                recv_sem=rsd.at[d],
                device_id={"lev": lev - d - 1},
                device_id_type=MESH,
            ).wait_recv()

    each(levels - 1, mass_wait)
    higher = jnp.sum(jnp.sum(recvd[...], axis=0), axis=0)
    left = jnp.concatenate(
        [
            jnp.concatenate([got[0:4], higher[0:1], jnp.zeros((3, wl), jnp.float32)], axis=0),
            jnp.concatenate([got[4:8], higher[1:2], jnp.zeros((3, wl), jnp.float32)], axis=0),
        ],
        axis=1,
    )
    grid = split_dot(left, thigh[...], tlow[...], ((1,), (1,)))
    q = qs[...]
    lon_step = 2.0 * math.pi / length
    lat_step = math.pi / (slots * n)
    flux = grid[0:1] * q
    ahead = jnp.concatenate([flux[:, 1:], flux[:, :1]], axis=1)
    behind = jnp.concatenate([flux[:, -1:], flux[:, :-1]], axis=1)
    zonal = (ahead - behind) * (1.0 / (2.0 * lon_step))

    for axis, place, count, step, k in halos:

        @pl.when(sends(place, count, -step))
        def _():
            halo_copy(axis, place, -step, k).wait_recv()

    merid = (grid[2:3] * qn[1] - grid[1:2] * qn[0]) * (1.0 / (2.0 * lat_step))
    sine = sine_ref[...].reshape(1, 1)
    base = (zonal + merid) / (1.0 - sine * sine)
    layer = grid[3:4] * thick
    above = qn[2]
    below = qn[3]

    prefix = grid[4:5]
    omega_bottom = -(prefix + layer)
    omega_top = -prefix
    vertical = (omega_bottom * (q + below) * 0.5 - omega_top * (above + q) * 0.5) / thick
    tendency = -weight_ref[...].reshape(1, 1) * (base + vertical)

    spectra = split_dot(tendency, thigh[...], tlow[...], ((1,), (0,))) * (2.0 / length)
    spectra = jnp.concatenate([spectra[:, :wl], spectra[:, wl:]], axis=0)

    def second(d):
        return wave_copy(send2, recv2, ss2, rs2, d, d, me)

    def second_start(d):
        shift = lax.rem(wl + me - lax.rem(me + d + 1, n), wl)
        send2[d] = pltpu.roll(spectra, shift, 1)
        second(d).start()

    each(n - 1, second_start)
    recv2[me] = spectra

    def second_wait(d):
        source = lax.rem(me - d - 1 + n, n)
        pltpu.make_async_remote_copy(
            src_ref=send2.at[d],
            dst_ref=recv2.at[source],
            send_sem=ss2.at[d],
            recv_sem=rs2.at[d],
            device_id={"wave": source},
            device_id_type=MESH,
        ).wait_recv()

    each(n - 1, second_wait)
    lane2 = lax.broadcasted_iota(jnp.int32, (2 * tracers, wl), 1)
    row_of = lax.rem(lane2, n)
    gathered = jnp.zeros((2 * tracers, wl), jnp.float32)
    if n <= 16:
        for i in range(n):
            gathered = jnp.where(row_of == i, recv2[i], gathered)
    else:
        gathered = lax.fori_loop(
            0, n, lambda i, g: jnp.where(row_of == i, recv2[i], g), gathered
        )
    lane3 = lax.broadcasted_iota(jnp.int32, (sp, wl), 1)
    sub3 = lax.broadcasted_iota(jnp.int32, (sp, wl), 0)
    own = (lane3 >= sub3 * n) & (lane3 < sub3 * n + n)
    blocks = []
    for c in range(tracers):
        for r in range(2):
            i = r * tracers + c
            blocks.append(jnp.where(own, gathered[i : i + 1], 0.0))
    left = jnp.concatenate(blocks, axis=0)[:, : slots * n]
    result = split_dot(left, lhigh[...], llow[...], ((1,), (0,)))
    for c in range(tracers):
        for r in range(2):
            at = (c * 2 + r) * sp
            out_ref[c, r, :, 0, :] = result[at : at + slots]

    each(n - 1, lambda d: first(d).wait_send())
    each(n - 1, lambda d: second(d).wait_send())
    for axis, place, count, step, k in halos:

        @pl.when(sends(place, count, step))
        def _():
            halo_copy(axis, place, step, k).wait_send()

    def mass_sent(d):
        @pl.when(lev + d + 1 < levels)
        def _():
            pltpu.make_async_remote_copy(
                src_ref=dmsg,
                dst_ref=recvd.at[lev],
                send_sem=ssd.at[d],
                recv_sem=rsd.at[d],
                device_id={"lev": lev + d + 1},
                device_id_type=MESH,
            ).wait_send()

    each(levels - 1, mass_sent)


def shards(vort_div, legendre, owner_map, lat_sine, quad_weight, thickness, tracers):
    slots, lat, degrees = legendre.shape
    count, own_levels, own_rows, length = tracers.shape
    n, levels = lax.axis_size("wave"), lax.axis_size("lev")
    assert own_levels == 1 and own_rows == 1 and lat == n
    wl = up_to(slots * n, 128)
    nd = up_to(degrees, 128)
    sp = up_to(slots, 8)
    f32 = jnp.float32
    bf16 = jnp.bfloat16
    operands = (
        jnp.transpose(vort_div, (0, 2, 1, 3)),
        legendre,
        owner_map.reshape(1, -1),
        lat_sine,
        quad_weight,
        thickness,
        tracers,
    )
    shapes = [
        ((4, sp, nd), f32),
        ((length, 2 * wl), bf16),
        ((length, 2 * wl), bf16),
        ((slots * lat, degrees), bf16),
        ((slots * lat, degrees), bf16),
        ((n, 8, wl), f32),
        ((n, 8, wl), f32),
        ((count, length), f32),
        ((4, count, length), f32),
        ((n, 2, wl), f32),
        ((levels, n, 2, wl), f32),
        ((n - 1, 2 * count, wl), f32),
        ((n, 2 * count, wl), f32),
    ]
    dma = pltpu.SemaphoreType.DMA
    scratch_bytes = sum(4 * math.prod(shape) for shape, _ in shapes)
    result = pl.pallas_call(
        functools.partial(kernel, n, levels, (slots, lat, degrees, length, count)),
        out_shape=jax.ShapeDtypeStruct((count, 2, slots, 1, degrees), f32),
        in_specs=[pl.BlockSpec(memory_space=pltpu.VMEM)] * len(operands),
        out_specs=pl.BlockSpec(memory_space=pltpu.VMEM),
        scratch_shapes=[pltpu.VMEM(shape, kind) for shape, kind in shapes]
        + [dma((n - 1,)), dma((n - 1,)), dma((4,)), dma((4,))]
        + [dma((levels - 1,)), dma((levels - 1,)), dma((n - 1,)), dma((n - 1,))],
        compiler_params=pltpu.CompilerParams(
            collective_id=0,
            has_side_effects=True,
            vmem_limit_bytes=min(2 * scratch_bytes + (8 << 20), 60 << 20),
        ),
    )(*operands)
    return jnp.transpose(result, (0, 1, 3, 2, 4))


def solution(mesh):
    placed = (
        P(None, "lev", "wave", None),
        P("wave", None, None),
        P(),
        P("wave"),
        P("wave"),
        P("lev"),
        P(None, "lev", "wave", None),
    )
    return jax.shard_map(
        shards,
        mesh=mesh,
        in_specs=placed,
        out_specs=P(None, None, "lev", "wave", None),
        check_vma=False,
    )
```

```python
import functools
import math

import jax
import jax.numpy as jnp
from jax import lax
from jax.experimental import pallas as pl
from jax.experimental.pallas import tpu as pltpu
from jax.sharding import PartitionSpec as P

planet_radius = 20.0
MESH = pl.DeviceIdType.MESH


def up_to(size, unit):
    return -(-size // unit) * unit


def each(count, body):
    if count <= 32:
        for i in range(count):
            body(i)
    else:

        def step(i, carry):
            body(i)
            return carry

        lax.fori_loop(0, count, step, 0)


def halves(x):
    high = x.astype(jnp.bfloat16).astype(jnp.float32)
    return high, x - high


def split_dot(left, right_high, right_low, dims):
    rows = left.shape[0]
    high, low = halves(left)
    both = jnp.concatenate([high, low], axis=0).astype(jnp.bfloat16)
    dot = functools.partial(
        lax.dot_general, dimension_numbers=(dims, ((), ())), preferred_element_type=jnp.float32
    )
    first = dot(both, right_high)
    return first[:rows] + first[rows:] + dot(high.astype(jnp.bfloat16), right_low)


def small_sin(x):
    y = x * x
    total = jnp.full_like(y, 1.0 / 6227020800.0)
    for c in (-1.0 / 39916800.0, 1.0 / 362880.0, -1.0 / 5040.0, 1.0 / 120.0, -1.0 / 6.0, 1.0):
        total = total * y + c
    return total * x


def kernel(
    n, levels, sizes,
    vd_ref, leg_ref, owner_ref, sine_ref, weight_ref, thick_ref, q_ref,
    out_ref,
    vdp, thigh, tlow, lhigh, llow, msg, recv1, qs, qn, dmsg, recvd, send2, recv2,
    ss1, rs1, ssq, rsq, ssd, rsd, ss2, rs2,
):
    slots, lat, degrees, length, tracers = sizes
    wl = thigh.shape[1] // 2
    nd = vdp.shape[2]
    sp = vdp.shape[1]
    me = lax.axis_index("wave")
    lev = lax.axis_index("lev")

    qn[...] = jnp.zeros_like(qn)
    recvd[...] = jnp.zeros_like(recvd)

    barrier = pltpu.get_barrier_semaphore()

    def greet_wave(d):
        pl.semaphore_signal(
            barrier, inc=1, device_id={"wave": lax.rem(me + d + 1, n)}, device_id_type=MESH
        )

    def greet_lev(d):
        pl.semaphore_signal(
            barrier, inc=1, device_id={"lev": lax.rem(lev + d + 1, levels)}, device_id_type=MESH
        )

    each(levels - 1, greet_lev)
    each(n - 1, greet_wave)

    vdp[...] = jnp.zeros_like(vdp)
    for f in range(4):
        vdp[f, :slots, :degrees] = vd_ref[f, 0]
    qs[...] = q_ref[:, 0, 0, :]
    owner = owner_ref[...].astype(jnp.float32)
    total_slots = owner.shape[1]
    place_at = lax.broadcasted_iota(jnp.int32, (sp, total_slots), 1)
    slot_at = lax.broadcasted_iota(jnp.int32, (sp, total_slots), 0)
    own_order = jnp.sum(
        jnp.where(place_at == me * slots + slot_at, owner, 0.0), axis=1, keepdims=True
    )
    thick = thick_ref[...].reshape(1, 1)
    sub = lax.broadcasted_iota(jnp.int32, (sp, nd), 0)
    degree = lax.broadcasted_iota(jnp.int32, (sp, nd), 1).astype(jnp.float32)
    order = jnp.where(sub < slots, own_order, 0.0)

    def coupling_at(d):
        ratio = jnp.maximum(d * d - order * order, 0.0) / jnp.maximum(4.0 * d * d - 1.0, 1.0)
        return jnp.where((d > order) & (d < degrees), jnp.sqrt(ratio), 0.0)

    lower_factor = -(degree - 1.0) * coupling_at(degree)
    upper_factor = (degree + 2.0) * coupling_at(degree + 1.0)
    inverse = jnp.where(
        degree > 0, -planet_radius * planet_radius / jnp.maximum(degree * (degree + 1.0), 1.0), 0.0
    )

    def derivative(field):
        return lower_factor * pltpu.roll(field, 1, 1) + upper_factor * pltpu.roll(field, nd - 1, 1)

    stream_real = inverse * vdp[0]
    stream_imag = inverse * vdp[1]
    potential_real = inverse * vdp[2]
    potential_imag = inverse * vdp[3]
    scale = 1.0 / planet_radius
    valid = degree >= order
    coefficients = [
        jnp.where(valid, c, 0.0)
        for c in (
            (-order * potential_imag - derivative(stream_real)) * scale,
            (order * potential_real - derivative(stream_imag)) * scale,
            (-order * stream_imag + derivative(potential_real)) * scale,
            (order * stream_real + derivative(potential_imag)) * scale,
            vdp[2],
            vdp[3],
        )
    ]

    lane = lax.broadcasted_iota(jnp.int32, (lat, wl), 1)
    fourier = [jnp.zeros((lat, wl), jnp.float32) for _ in range(6)]
    for s in range(slots):
        p_s = leg_ref[s]
        here = lane == s * n + me
        for f in range(6):
            total = jnp.sum(p_s * coefficients[f][s : s + 1, :degrees], axis=1, keepdims=True)
            fourier[f] = jnp.where(here, total, fourier[f])
    row = lax.broadcasted_iota(jnp.int32, (lat, wl), 0)

    def row_before(x):
        return jnp.where(row == 0, 0.0, pltpu.roll(x, 1, 0))

    def row_after(x):
        return jnp.where(row == lat - 1, 0.0, pltpu.roll(x, lat - 1, 0))

    for part in range(2):
        east, north, div = fourier[part], fourier[2 + part], fourier[4 + part]
        for t, value in enumerate((east, row_before(north), row_after(north), div)):
            msg[:, 4 * part + t, :] = value

    pl.semaphore_wait(barrier, n + levels - 2)

    def wave_copy(source, target, send, recv, d, buffer_at, out_at):
        return pltpu.make_async_remote_copy(
            src_ref=source.at[buffer_at],
            dst_ref=target.at[out_at],
            send_sem=send.at[d],
            recv_sem=recv.at[d],
            device_id={"wave": lax.rem(me + d + 1, n)},
            device_id_type=MESH,
        )

    def first(d):
        return wave_copy(msg, recv1, ss1, rs1, d, lax.rem(me + d + 1, n), me)

    each(n - 1, lambda d: first(d).start())

    halos = (
        ("wave", me, n, 1, 0),
        ("wave", me, n, -1, 1),
        ("lev", lev, levels, 1, 2),
        ("lev", lev, levels, -1, 3),
    )

    def halo_copy(axis, place, step, k):
        return pltpu.make_async_remote_copy(
            src_ref=qs,
            dst_ref=qn.at[k],
            send_sem=ssq.at[k],
            recv_sem=rsq.at[k],
            device_id={axis: place + step},
            device_id_type=MESH,
        )

    def sends(place, count, step):
        return place < count - 1 if step > 0 else place > 0

    for axis, place, count, step, k in halos:

        @pl.when(sends(place, count, step))
        def _():
            halo_copy(axis, place, step, k).start()

    lane1 = lax.broadcasted_iota(jnp.int32, (1, wl), 1)
    target = lax.broadcasted_iota(jnp.int32, (wl, total_slots), 0)
    source_at = lax.broadcasted_iota(jnp.int32, (wl, total_slots), 1)
    column = jnp.sum(
        jnp.where(source_at == lax.rem(target, n) * slots + target // n, owner, 0.0),
        axis=1,
        keepdims=True,
    )
    square = (wl, wl)
    diagonal = lax.broadcasted_iota(jnp.int32, square, 0) == lax.broadcasted_iota(jnp.int32, square, 1)
    numbers = jnp.sum(jnp.where(diagonal, column, 0.0), axis=0, keepdims=True)
    filled = lane1 < slots * n
    block = 32 if length % 32 == 0 else 8 if length % 8 == 0 else length

    def table_block(b):
        start = b * block
        if not isinstance(b, int):
            start = pl.multiple_of(start, block)
        lon = lax.broadcasted_iota(jnp.int32, (block, wl), 0).astype(jnp.float32)
        if isinstance(b, int):
            lon = lon + float(start)
        else:
            lon = lon + start.astype(jnp.float32)
        product = numbers * lon
        turn = product - length * jnp.floor(product * (1.0 / length))
        turn = jnp.where(turn < 0, turn + length, turn)
        turn = jnp.where(turn >= length, turn - length, turn)
        turn = jnp.where(turn > length / 2, turn - length, turn)
        size = jnp.abs(turn)
        unit = 2.0 * math.pi / length
        cosine = small_sin((length / 4 - size) * unit)
        sine = small_sin(jnp.minimum(size, length / 2 - size) * unit)
        minus_sine = jnp.where(turn > 0, -sine, sine)
        for part, value in enumerate((cosine, minus_sine)):
            high, low = halves(jnp.where(filled, value, 0.0))
            at = (pl.ds(start, block), pl.ds(part * wl, wl))
            thigh[at] = high.astype(jnp.bfloat16)
            tlow[at] = low.astype(jnp.bfloat16)

    each(length // block, table_block)
    degree_row = lax.broadcasted_iota(jnp.int32, (lat, degrees), 1).astype(jnp.float32)
    masked = jnp.concatenate(
        [jnp.where(degree_row >= own_order[s : s + 1], leg_ref[s], 0.0) for s in range(slots)], axis=0
    )
    high, low = halves(masked)
    lhigh[...] = high.astype(jnp.bfloat16)
    llow[...] = low.astype(jnp.bfloat16)

    recv1[me] = msg[me]

    def first_wait(d):
        source = lax.rem(me - d - 1 + n, n)
        pltpu.make_async_remote_copy(
            src_ref=msg.at[0],
            dst_ref=recv1.at[source],
            send_sem=ss1.at[d],
            recv_sem=rs1.at[d],
            device_id={"wave": source},
            device_id_type=MESH,
        ).wait_recv()

    each(n - 1, first_wait)
    got = jnp.sum(recv1[...], axis=0)

    dmsg[0:1, :] = got[3:4] * thick
    dmsg[1:2, :] = got[7:8] * thick

    def mass(d):
        return pltpu.make_async_remote_copy(
            src_ref=dmsg,
            dst_ref=recvd.at[lev],
            send_sem=ssd.at[d],
            recv_sem=rsd.at[d],
            device_id={"lev": lev + d + 1},
            device_id_type=MESH,
        )

    def mass_start(d):
        @pl.when(lev + d + 1 < levels)
        def _():
            mass(d).start()

    each(levels - 1, mass_start)
    left = jnp.concatenate([got[0:4], got[4:8]], axis=1)
    grid = split_dot(left, thigh[...], tlow[...], ((1,), (1,)))
    q = qs[...]
    lon_step = 2.0 * math.pi / length
    lat_step = math.pi / (slots * n)
    flux = grid[0:1] * q
    ahead = jnp.concatenate([flux[:, 1:], flux[:, :1]], axis=1)
    behind = jnp.concatenate([flux[:, -1:], flux[:, :-1]], axis=1)
    zonal = (ahead - behind) * (1.0 / (2.0 * lon_step))

    for axis, place, count, step, k in halos:

        @pl.when(sends(place, count, -step))
        def _():
            halo_copy(axis, place, -step, k).wait_recv()

    merid = (grid[2:3] * qn[1] - grid[1:2] * qn[0]) * (1.0 / (2.0 * lat_step))
    sine = sine_ref[...].reshape(1, 1)
    base = (zonal + merid) / (1.0 - sine * sine)
    layer = grid[3:4] * thick
    above = qn[2]
    below = qn[3]


    def mass_wait(d):
        @pl.when(lev - d - 1 >= 0)
        def _():
            pltpu.make_async_remote_copy(
                src_ref=dmsg,
                dst_ref=recvd.at[lev - d - 1],
                send_sem=ssd.at[d],
                recv_sem=rsd.at[d],
                device_id={"lev": lev - d - 1},
                device_id_type=MESH,
            ).wait_recv()

    each(levels - 1, mass_wait)
    higher = jnp.sum(recvd[...], axis=0)
    left = jnp.concatenate([higher[0:1], higher[1:2]], axis=1)
    prefix = split_dot(left, thigh[...], tlow[...], ((1,), (1,)))
    omega_bottom = -(prefix + layer)
    omega_top = -prefix
    vertical = (omega_bottom * (q + below) * 0.5 - omega_top * (above + q) * 0.5) / thick
    tendency = -weight_ref[...].reshape(1, 1) * (base + vertical)

    spectra = split_dot(tendency, thigh[...], tlow[...], ((1,), (0,))) * (2.0 / length)
    spectra = jnp.concatenate([spectra[:, :wl], spectra[:, wl:]], axis=0)

    def second(d):
        return wave_copy(send2, recv2, ss2, rs2, d, d, me)

    def second_start(d):
        shift = lax.rem(wl + me - lax.rem(me + d + 1, n), wl)
        send2[d] = pltpu.roll(spectra, shift, 1)
        second(d).start()

    each(n - 1, second_start)
    recv2[me] = spectra

    def second_wait(d):
        source = lax.rem(me - d - 1 + n, n)
        pltpu.make_async_remote_copy(
            src_ref=send2.at[d],
            dst_ref=recv2.at[source],
            send_sem=ss2.at[d],
            recv_sem=rs2.at[d],
            device_id={"wave": source},
            device_id_type=MESH,
        ).wait_recv()

    each(n - 1, second_wait)
    lane2 = lax.broadcasted_iota(jnp.int32, (2 * tracers, wl), 1)
    row_of = lax.rem(lane2, n)
    gathered = jnp.zeros((2 * tracers, wl), jnp.float32)
    if n <= 16:
        for i in range(n):
            gathered = jnp.where(row_of == i, recv2[i], gathered)
    else:
        gathered = lax.fori_loop(
            0, n, lambda i, g: jnp.where(row_of == i, recv2[i], g), gathered
        )
    lane3 = lax.broadcasted_iota(jnp.int32, (sp, wl), 1)
    sub3 = lax.broadcasted_iota(jnp.int32, (sp, wl), 0)
    own = (lane3 >= sub3 * n) & (lane3 < sub3 * n + n)
    blocks = []
    for c in range(tracers):
        for r in range(2):
            i = r * tracers + c
            blocks.append(jnp.where(own, gathered[i : i + 1], 0.0))
    left = jnp.concatenate(blocks, axis=0)[:, : slots * n]
    result = split_dot(left, lhigh[...], llow[...], ((1,), (0,)))
    for c in range(tracers):
        for r in range(2):
            at = (c * 2 + r) * sp
            out_ref[c, r, :, 0, :] = result[at : at + slots]

    each(n - 1, lambda d: first(d).wait_send())
    each(n - 1, lambda d: second(d).wait_send())
    for axis, place, count, step, k in halos:

        @pl.when(sends(place, count, step))
        def _():
            halo_copy(axis, place, step, k).wait_send()

    def mass_sent(d):
        @pl.when(lev + d + 1 < levels)
        def _():
            mass(d).wait_send()

    each(levels - 1, mass_sent)


def shards(vort_div, legendre, owner_map, lat_sine, quad_weight, thickness, tracers):
    slots, lat, degrees = legendre.shape
    count, own_levels, own_rows, length = tracers.shape
    n, levels = lax.axis_size("wave"), lax.axis_size("lev")
    assert own_levels == 1 and own_rows == 1 and lat == n
    wl = up_to(slots * n, 128)
    nd = up_to(degrees, 128)
    sp = up_to(slots, 8)
    f32 = jnp.float32
    bf16 = jnp.bfloat16
    operands = (
        vort_div,
        legendre,
        owner_map.reshape(1, -1),
        lat_sine,
        quad_weight,
        thickness,
        tracers,
    )
    shapes = [
        ((4, sp, nd), f32),
        ((length, 2 * wl), bf16),
        ((length, 2 * wl), bf16),
        ((slots * lat, degrees), bf16),
        ((slots * lat, degrees), bf16),
        ((n, 8, wl), f32),
        ((n, 8, wl), f32),
        ((count, length), f32),
        ((4, count, length), f32),
        ((2, wl), f32),
        ((levels, 2, wl), f32),
        ((n - 1, 2 * count, wl), f32),
        ((n, 2 * count, wl), f32),
    ]
    dma = pltpu.SemaphoreType.DMA
    scratch_bytes = sum(4 * math.prod(shape) for shape, _ in shapes)
    result = pl.pallas_call(
        functools.partial(kernel, n, levels, (slots, lat, degrees, length, count)),
        out_shape=jax.ShapeDtypeStruct((count, 2, slots, 1, degrees), f32),
        in_specs=[pl.BlockSpec(memory_space=pltpu.VMEM)] * len(operands),
        out_specs=pl.BlockSpec(memory_space=pltpu.VMEM),
        scratch_shapes=[pltpu.VMEM(shape, kind) for shape, kind in shapes]
        + [dma((n - 1,)), dma((n - 1,)), dma((4,)), dma((4,))]
        + [dma((levels - 1,)), dma((levels - 1,)), dma((n - 1,)), dma((n - 1,))],
        compiler_params=pltpu.CompilerParams(
            collective_id=0,
            has_side_effects=True,
            vmem_limit_bytes=min(2 * scratch_bytes + (8 << 20), 60 << 20),
        ),
    )(*operands)
    return jnp.transpose(result, (0, 1, 3, 2, 4))


def solution(mesh):
    placed = (
        P(None, "lev", "wave", None),
        P("wave", None, None),
        P(),
        P("wave"),
        P("wave"),
        P("lev"),
        P(None, "lev", "wave", None),
    )
    return jax.shard_map(
        shards,
        mesh=mesh,
        in_specs=placed,
        out_specs=P(None, None, "lev", "wave", None),
        check_vma=False,
    )
```

```python
import functools
import math

import jax
import jax.numpy as jnp
from jax import lax
from jax.experimental import pallas as pl
from jax.experimental.pallas import tpu as pltpu
from jax.sharding import PartitionSpec as P

planet_radius = 20.0
MESH = pl.DeviceIdType.MESH


def up_to(size, unit):
    return -(-size // unit) * unit


def each(count, body):
    if count <= 32:
        for i in range(count):
            body(i)
    else:

        def step(i, carry):
            body(i)
            return carry

        lax.fori_loop(0, count, step, 0)


def halves(x):
    high = x.astype(jnp.bfloat16).astype(jnp.float32)
    return high, x - high


def split_dot(left, right_high, right_low, dims):
    rows = left.shape[0]
    high, low = halves(left)
    both = jnp.concatenate([high, low], axis=0).astype(jnp.bfloat16)
    dot = functools.partial(
        lax.dot_general, dimension_numbers=(dims, ((), ())), preferred_element_type=jnp.float32
    )
    first = dot(both, right_high)
    return first[:rows] + first[rows:] + dot(high.astype(jnp.bfloat16), right_low)


def small_sin(x):
    y = x * x
    total = jnp.full_like(y, 1.0 / 6227020800.0)
    for c in (-1.0 / 39916800.0, 1.0 / 362880.0, -1.0 / 5040.0, 1.0 / 120.0, -1.0 / 6.0, 1.0):
        total = total * y + c
    return total * x


def kernel(
    n, levels, sizes,
    vd_ref, leg_ref, owner_ref, sine_ref, weight_ref, thick_ref, q_ref,
    out_ref,
    vdp, thigh, tlow, lhigh, llow, msg, recv1, qs, qn, dmsg, recvd, send2, recv2,
    ss1, rs1, ssq, rsq, ssd, rsd, ss2, rs2,
):
    slots, lat, degrees, length, tracers = sizes
    wl = thigh.shape[1] // 2
    nd = vdp.shape[2]
    sp = vdp.shape[1]
    me = lax.axis_index("wave")
    lev = lax.axis_index("lev")

    qn[...] = jnp.zeros_like(qn)
    recvd[...] = jnp.zeros_like(recvd)

    barrier = pltpu.get_barrier_semaphore()

    def greet_wave(d):
        pl.semaphore_signal(
            barrier, inc=1, device_id={"wave": lax.rem(me + d + 1, n)}, device_id_type=MESH
        )

    def greet_lev(d):
        pl.semaphore_signal(
            barrier, inc=1, device_id={"lev": lax.rem(lev + d + 1, levels)}, device_id_type=MESH
        )

    each(levels - 1, greet_lev)
    each(n - 1, greet_wave)

    vdp[...] = jnp.zeros_like(vdp)
    for f in range(4):
        vdp[f, :slots, :degrees] = vd_ref[f, 0]
    qs[...] = q_ref[:, 0, 0, :]
    owner = owner_ref[...].astype(jnp.float32)
    total_slots = owner.shape[1]
    place_at = lax.broadcasted_iota(jnp.int32, (sp, total_slots), 1)
    slot_at = lax.broadcasted_iota(jnp.int32, (sp, total_slots), 0)
    own_order = jnp.sum(
        jnp.where(place_at == me * slots + slot_at, owner, 0.0), axis=1, keepdims=True
    )
    thick = jnp.full((1, 1), thick_ref[0], jnp.float32)
    sub = lax.broadcasted_iota(jnp.int32, (sp, nd), 0)
    degree = lax.broadcasted_iota(jnp.int32, (sp, nd), 1).astype(jnp.float32)
    order = jnp.where(sub < slots, own_order, 0.0)

    def coupling_at(d):
        ratio = jnp.maximum(d * d - order * order, 0.0) / jnp.maximum(4.0 * d * d - 1.0, 1.0)
        return jnp.where((d > order) & (d < degrees), jnp.sqrt(ratio), 0.0)

    lower_factor = -(degree - 1.0) * coupling_at(degree)
    upper_factor = (degree + 2.0) * coupling_at(degree + 1.0)
    inverse = jnp.where(
        degree > 0, -planet_radius * planet_radius / jnp.maximum(degree * (degree + 1.0), 1.0), 0.0
    )

    def derivative(field):
        return lower_factor * pltpu.roll(field, 1, 1) + upper_factor * pltpu.roll(field, nd - 1, 1)

    stream_real = inverse * vdp[0]
    stream_imag = inverse * vdp[1]
    potential_real = inverse * vdp[2]
    potential_imag = inverse * vdp[3]
    scale = 1.0 / planet_radius
    valid = degree >= order
    coefficients = [
        jnp.where(valid, c, 0.0)
        for c in (
            (-order * potential_imag - derivative(stream_real)) * scale,
            (order * potential_real - derivative(stream_imag)) * scale,
            (-order * stream_imag + derivative(potential_real)) * scale,
            (order * stream_real + derivative(potential_imag)) * scale,
            vdp[2],
            vdp[3],
        )
    ]

    lane = lax.broadcasted_iota(jnp.int32, (lat, wl), 1)
    fourier = [jnp.zeros((lat, wl), jnp.float32) for _ in range(6)]
    for s in range(slots):
        p_s = leg_ref[s]
        here = lane == s * n + me
        for f in range(6):
            total = jnp.sum(p_s * coefficients[f][s : s + 1, :degrees], axis=1, keepdims=True)
            fourier[f] = jnp.where(here, total, fourier[f])
    row = lax.broadcasted_iota(jnp.int32, (lat, wl), 0)

    def row_before(x):
        return jnp.where(row == 0, 0.0, pltpu.roll(x, 1, 0))

    def row_after(x):
        return jnp.where(row == lat - 1, 0.0, pltpu.roll(x, lat - 1, 0))

    for part in range(2):
        east, north, div = fourier[part], fourier[2 + part], fourier[4 + part]
        for t, value in enumerate((east, row_before(north), row_after(north), div)):
            msg[:, 4 * part + t, :] = value

    pl.semaphore_wait(barrier, n + levels - 2)

    def wave_copy(source, target, send, recv, d, buffer_at, out_at):
        return pltpu.make_async_remote_copy(
            src_ref=source.at[buffer_at],
            dst_ref=target.at[out_at],
            send_sem=send.at[d],
            recv_sem=recv.at[d],
            device_id={"wave": lax.rem(me + d + 1, n)},
            device_id_type=MESH,
        )

    def first(d):
        return wave_copy(msg, recv1, ss1, rs1, d, lax.rem(me + d + 1, n), me)

    each(n - 1, lambda d: first(d).start())

    halos = (
        ("wave", me, n, 1, 0),
        ("wave", me, n, -1, 1),
        ("lev", lev, levels, 1, 2),
        ("lev", lev, levels, -1, 3),
    )

    def halo_copy(axis, place, step, k):
        return pltpu.make_async_remote_copy(
            src_ref=qs,
            dst_ref=qn.at[k],
            send_sem=ssq.at[k],
            recv_sem=rsq.at[k],
            device_id={axis: place + step},
            device_id_type=MESH,
        )

    def sends(place, count, step):
        return place < count - 1 if step > 0 else place > 0

    for axis, place, count, step, k in halos:

        @pl.when(sends(place, count, step))
        def _():
            halo_copy(axis, place, step, k).start()

    lane1 = lax.broadcasted_iota(jnp.int32, (1, wl), 1)
    target = lax.broadcasted_iota(jnp.int32, (wl, total_slots), 0)
    source_at = lax.broadcasted_iota(jnp.int32, (wl, total_slots), 1)
    column = jnp.sum(
        jnp.where(source_at == lax.rem(target, n) * slots + target // n, owner, 0.0),
        axis=1,
        keepdims=True,
    )
    square = (wl, wl)
    diagonal = lax.broadcasted_iota(jnp.int32, square, 0) == lax.broadcasted_iota(jnp.int32, square, 1)
    numbers = jnp.sum(jnp.where(diagonal, column, 0.0), axis=0, keepdims=True)
    filled = lane1 < slots * n
    block = 32 if length % 32 == 0 else 8 if length % 8 == 0 else length

    def table_block(b):
        start = b * block
        if not isinstance(b, int):
            start = pl.multiple_of(start, block)
        lon = lax.broadcasted_iota(jnp.int32, (block, wl), 0).astype(jnp.float32)
        if isinstance(b, int):
            lon = lon + float(start)
        else:
            lon = lon + start.astype(jnp.float32)
        product = numbers * lon
        turn = product - length * jnp.floor(product * (1.0 / length))
        turn = jnp.where(turn < 0, turn + length, turn)
        turn = jnp.where(turn >= length, turn - length, turn)
        turn = jnp.where(turn > length / 2, turn - length, turn)
        size = jnp.abs(turn)
        unit = 2.0 * math.pi / length
        cosine = small_sin((length / 4 - size) * unit)
        sine = small_sin(jnp.minimum(size, length / 2 - size) * unit)
        minus_sine = jnp.where(turn > 0, -sine, sine)
        for part, value in enumerate((cosine, minus_sine)):
            high, low = halves(jnp.where(filled, value, 0.0))
            at = (pl.ds(start, block), pl.ds(part * wl, wl))
            thigh[at] = high.astype(jnp.bfloat16)
            tlow[at] = low.astype(jnp.bfloat16)

    each(length // block, table_block)
    degree_row = lax.broadcasted_iota(jnp.int32, (lat, degrees), 1).astype(jnp.float32)
    masked = jnp.concatenate(
        [jnp.where(degree_row >= own_order[s : s + 1], leg_ref[s], 0.0) for s in range(slots)], axis=0
    )
    high, low = halves(masked)
    lhigh[...] = high.astype(jnp.bfloat16)
    llow[...] = low.astype(jnp.bfloat16)

    recv1[me] = msg[me]

    def first_wait(d):
        source = lax.rem(me - d - 1 + n, n)
        pltpu.make_async_remote_copy(
            src_ref=msg.at[0],
            dst_ref=recv1.at[source],
            send_sem=ss1.at[d],
            recv_sem=rs1.at[d],
            device_id={"wave": source},
            device_id_type=MESH,
        ).wait_recv()

    each(n - 1, first_wait)
    got = jnp.sum(recv1[...], axis=0)

    dmsg[0:1, :] = got[3:4] * thick
    dmsg[1:2, :] = got[7:8] * thick

    def mass(d):
        return pltpu.make_async_remote_copy(
            src_ref=dmsg,
            dst_ref=recvd.at[lev],
            send_sem=ssd.at[d],
            recv_sem=rsd.at[d],
            device_id={"lev": lev + d + 1},
            device_id_type=MESH,
        )

    def mass_start(d):
        @pl.when(lev + d + 1 < levels)
        def _():
            mass(d).start()

    each(levels - 1, mass_start)
    left = jnp.concatenate([got[0:4], got[4:8]], axis=1)
    grid = split_dot(left, thigh[...], tlow[...], ((1,), (1,)))
    q = qs[...]
    lon_step = 2.0 * math.pi / length
    lat_step = math.pi / (slots * n)
    flux = grid[0:1] * q
    ahead = jnp.concatenate([flux[:, 1:], flux[:, :1]], axis=1)
    behind = jnp.concatenate([flux[:, -1:], flux[:, :-1]], axis=1)
    zonal = (ahead - behind) * (1.0 / (2.0 * lon_step))

    for axis, place, count, step, k in halos:

        @pl.when(sends(place, count, -step))
        def _():
            halo_copy(axis, place, -step, k).wait_recv()

    merid = (grid[2:3] * qn[1] - grid[1:2] * qn[0]) * (1.0 / (2.0 * lat_step))
    sine = jnp.full((1, 1), sine_ref[0], jnp.float32)
    base = (zonal + merid) / (1.0 - sine * sine)
    layer = grid[3:4] * thick
    above = qn[2]
    below = qn[3]


    def mass_wait(d):
        @pl.when(lev - d - 1 >= 0)
        def _():
            pltpu.make_async_remote_copy(
                src_ref=dmsg,
                dst_ref=recvd.at[lev - d - 1],
                send_sem=ssd.at[d],
                recv_sem=rsd.at[d],
                device_id={"lev": lev - d - 1},
                device_id_type=MESH,
            ).wait_recv()

    each(levels - 1, mass_wait)
    higher = jnp.sum(recvd[...], axis=0)
    left = jnp.concatenate([higher[0:1], higher[1:2]], axis=1)
    prefix = split_dot(left, thigh[...], tlow[...], ((1,), (1,)))
    omega_bottom = -(prefix + layer)
    omega_top = -prefix
    vertical = (omega_bottom * (q + below) * 0.5 - omega_top * (above + q) * 0.5) / thick
    tendency = -jnp.full((1, 1), weight_ref[0], jnp.float32) * (base + vertical)

    spectra = split_dot(tendency, thigh[...], tlow[...], ((1,), (0,))) * (2.0 / length)
    spectra = jnp.concatenate([spectra[:, :wl], spectra[:, wl:]], axis=0)

    def second(d):
        return wave_copy(send2, recv2, ss2, rs2, d, d, me)

    def second_start(d):
        shift = lax.rem(wl + me - lax.rem(me + d + 1, n), wl)
        send2[d] = pltpu.roll(spectra, shift, 1)
        second(d).start()

    each(n - 1, second_start)
    recv2[me] = spectra

    def second_wait(d):
        source = lax.rem(me - d - 1 + n, n)
        pltpu.make_async_remote_copy(
            src_ref=send2.at[d],
            dst_ref=recv2.at[source],
            send_sem=ss2.at[d],
            recv_sem=rs2.at[d],
            device_id={"wave": source},
            device_id_type=MESH,
        ).wait_recv()

    each(n - 1, second_wait)
    lane2 = lax.broadcasted_iota(jnp.int32, (2 * tracers, wl), 1)
    row_of = lax.rem(lane2, n)
    gathered = jnp.zeros((2 * tracers, wl), jnp.float32)
    if n <= 16:
        for i in range(n):
            gathered = jnp.where(row_of == i, recv2[i], gathered)
    else:
        gathered = lax.fori_loop(
            0, n, lambda i, g: jnp.where(row_of == i, recv2[i], g), gathered
        )
    lane3 = lax.broadcasted_iota(jnp.int32, (sp, wl), 1)
    sub3 = lax.broadcasted_iota(jnp.int32, (sp, wl), 0)
    own = (lane3 >= sub3 * n) & (lane3 < sub3 * n + n)
    blocks = []
    for c in range(tracers):
        for r in range(2):
            i = r * tracers + c
            blocks.append(jnp.where(own, gathered[i : i + 1], 0.0))
    left = jnp.concatenate(blocks, axis=0)[:, : slots * n]
    result = split_dot(left, lhigh[...], llow[...], ((1,), (0,)))
    for c in range(tracers):
        for r in range(2):
            at = (c * 2 + r) * sp
            out_ref[c, r, :, 0, :] = result[at : at + slots]

    each(n - 1, lambda d: first(d).wait_send())
    each(n - 1, lambda d: second(d).wait_send())
    for axis, place, count, step, k in halos:

        @pl.when(sends(place, count, step))
        def _():
            halo_copy(axis, place, step, k).wait_send()

    def mass_sent(d):
        @pl.when(lev + d + 1 < levels)
        def _():
            mass(d).wait_send()

    each(levels - 1, mass_sent)


def shards(vort_div, legendre, owner_map, lat_sine, quad_weight, thickness, tracers):
    slots, lat, degrees = legendre.shape
    count, own_levels, own_rows, length = tracers.shape
    n, levels = lax.axis_size("wave"), lax.axis_size("lev")
    assert own_levels == 1 and own_rows == 1 and lat == n
    wl = up_to(slots * n, 128)
    nd = up_to(degrees, 128)
    sp = up_to(slots, 8)
    f32 = jnp.float32
    bf16 = jnp.bfloat16
    operands = (
        vort_div,
        legendre,
        owner_map.reshape(1, -1),
        lat_sine,
        quad_weight,
        thickness,
        tracers,
    )
    shapes = [
        ((4, sp, nd), f32),
        ((length, 2 * wl), bf16),
        ((length, 2 * wl), bf16),
        ((slots * lat, degrees), bf16),
        ((slots * lat, degrees), bf16),
        ((n, 8, wl), f32),
        ((n, 8, wl), f32),
        ((count, length), f32),
        ((4, count, length), f32),
        ((2, wl), f32),
        ((levels, 2, wl), f32),
        ((n - 1, 2 * count, wl), f32),
        ((n, 2 * count, wl), f32),
    ]
    dma = pltpu.SemaphoreType.DMA
    scratch_bytes = sum(4 * math.prod(shape) for shape, _ in shapes)
    result = pl.pallas_call(
        functools.partial(kernel, n, levels, (slots, lat, degrees, length, count)),
        out_shape=jax.ShapeDtypeStruct((count, 2, slots, 1, degrees), f32),
        in_specs=[
            pl.BlockSpec(memory_space=pltpu.SMEM if x.shape == (1,) else pltpu.VMEM) for x in operands
        ],
        out_specs=pl.BlockSpec(memory_space=pltpu.VMEM),
        scratch_shapes=[pltpu.VMEM(shape, kind) for shape, kind in shapes]
        + [dma((n - 1,)), dma((n - 1,)), dma((4,)), dma((4,))]
        + [dma((levels - 1,)), dma((levels - 1,)), dma((n - 1,)), dma((n - 1,))],
        compiler_params=pltpu.CompilerParams(
            collective_id=0,
            has_side_effects=True,
            vmem_limit_bytes=min(2 * scratch_bytes + (8 << 20), 60 << 20),
        ),
    )(*operands)
    return jnp.transpose(result, (0, 1, 3, 2, 4))


def solution(mesh):
    placed = (
        P(None, "lev", "wave", None),
        P("wave", None, None),
        P(),
        P("wave"),
        P("wave"),
        P("lev"),
        P(None, "lev", "wave", None),
    )
    return jax.shard_map(
        shards,
        mesh=mesh,
        in_specs=placed,
        out_specs=P(None, None, "lev", "wave", None),
        check_vma=False,
    )
```

```python
import functools
import math

import jax
import jax.numpy as jnp
from jax import lax
from jax.experimental import pallas as pl
from jax.experimental.pallas import tpu as pltpu
from jax.sharding import PartitionSpec as P

planet_radius = 20.0
MESH = pl.DeviceIdType.MESH


def up_to(size, unit):
    return -(-size // unit) * unit


def each(count, body):
    if count <= 32:
        for i in range(count):
            body(i)
    else:

        def step(i, carry):
            body(i)
            return carry

        lax.fori_loop(0, count, step, 0)


def halves(x):
    high = x.astype(jnp.bfloat16).astype(jnp.float32)
    return high, x - high


def split_dot(left, right_high, right_low, dims):
    rows = left.shape[0]
    high, low = halves(left)
    both = jnp.concatenate([high, low], axis=0).astype(jnp.bfloat16)
    dot = functools.partial(
        lax.dot_general, dimension_numbers=(dims, ((), ())), preferred_element_type=jnp.float32
    )
    first = dot(both, right_high)
    return first[:rows] + first[rows:] + dot(high.astype(jnp.bfloat16), right_low)


def small_sin(x):
    y = x * x
    total = jnp.full_like(y, 1.0 / 6227020800.0)
    for c in (-1.0 / 39916800.0, 1.0 / 362880.0, -1.0 / 5040.0, 1.0 / 120.0, -1.0 / 6.0, 1.0):
        total = total * y + c
    return total * x


def kernel(
    n, levels, sizes,
    vd_ref, leg_ref, owner_ref, sine_ref, weight_ref, thick_ref, q_ref,
    out_ref,
    vdp, thigh, tlow, lhigh, llow, msg, recv1, qs, qn, dmsg, recvd, send2, recv2,
    ss1, rs1, ssq, rsq, ssd, rsd, ss2, rs2,
):
    slots, lat, degrees, length, tracers = sizes
    wl = thigh.shape[1] // 2
    nd = vdp.shape[2]
    sp = vdp.shape[1]
    me = lax.axis_index("wave")
    lev = lax.axis_index("lev")

    qn[...] = jnp.zeros_like(qn)
    recvd[...] = jnp.zeros_like(recvd)

    barrier = pltpu.get_barrier_semaphore()

    def greet_wave(d):
        pl.semaphore_signal(
            barrier, inc=1, device_id={"wave": lax.rem(me + d + 1, n)}, device_id_type=MESH
        )

    def greet_lev(d):
        pl.semaphore_signal(
            barrier, inc=1, device_id={"lev": lax.rem(lev + d + 1, levels)}, device_id_type=MESH
        )

    each(levels - 1, greet_lev)
    each(n - 1, greet_wave)

    vdp[...] = jnp.zeros_like(vdp)
    for f in range(4):
        vdp[f, :slots, :degrees] = vd_ref[f, 0]
    qs[...] = q_ref[:, 0, 0, :]
    owner = owner_ref[...].astype(jnp.float32)
    total_slots = owner.shape[1]
    place_at = lax.broadcasted_iota(jnp.int32, (sp, total_slots), 1)
    slot_at = lax.broadcasted_iota(jnp.int32, (sp, total_slots), 0)
    own_order = jnp.sum(
        jnp.where(place_at == me * slots + slot_at, owner, 0.0), axis=1, keepdims=True
    )
    thick = jnp.full((1, 1), thick_ref[0], jnp.float32)
    sub = lax.broadcasted_iota(jnp.int32, (sp, nd), 0)
    degree = lax.broadcasted_iota(jnp.int32, (sp, nd), 1).astype(jnp.float32)
    order = jnp.where(sub < slots, own_order, 0.0)

    def coupling_at(d):
        ratio = jnp.maximum(d * d - order * order, 0.0) / jnp.maximum(4.0 * d * d - 1.0, 1.0)
        return jnp.where((d > order) & (d < degrees), jnp.sqrt(ratio), 0.0)

    lower_factor = -(degree - 1.0) * coupling_at(degree)
    upper_factor = (degree + 2.0) * coupling_at(degree + 1.0)
    inverse = jnp.where(
        degree > 0, -planet_radius * planet_radius / jnp.maximum(degree * (degree + 1.0), 1.0), 0.0
    )

    def derivative(field):
        return lower_factor * pltpu.roll(field, 1, 1) + upper_factor * pltpu.roll(field, nd - 1, 1)

    stream_real = inverse * vdp[0]
    stream_imag = inverse * vdp[1]
    potential_real = inverse * vdp[2]
    potential_imag = inverse * vdp[3]
    scale = 1.0 / planet_radius
    valid = degree >= order
    coefficients = [
        jnp.where(valid, c, 0.0)
        for c in (
            (-order * potential_imag - derivative(stream_real)) * scale,
            (order * potential_real - derivative(stream_imag)) * scale,
            (-order * stream_imag + derivative(potential_real)) * scale,
            (order * stream_real + derivative(potential_imag)) * scale,
            vdp[2],
            vdp[3],
        )
    ]

    lane = lax.broadcasted_iota(jnp.int32, (lat, wl), 1)
    fourier = [jnp.zeros((lat, wl), jnp.float32) for _ in range(6)]
    for s in range(slots):
        p_s = leg_ref[s]
        here = lane == s * n + me
        for f in range(6):
            total = jnp.sum(p_s * coefficients[f][s : s + 1, :degrees], axis=1, keepdims=True)
            fourier[f] = jnp.where(here, total, fourier[f])
    row = lax.broadcasted_iota(jnp.int32, (lat, wl), 0)

    def row_before(x):
        return jnp.where(row == 0, 0.0, pltpu.roll(x, 1, 0))

    def row_after(x):
        return jnp.where(row == lat - 1, 0.0, pltpu.roll(x, lat - 1, 0))

    for part in range(2):
        east, north, div = fourier[part], fourier[2 + part], fourier[4 + part]
        for t, value in enumerate((east, row_before(north), row_after(north), div)):
            msg[:, 4 * part + t, :] = value

    pl.semaphore_wait(barrier, n + levels - 2)

    def wave_copy(source, target, send, recv, d, buffer_at, out_at):
        return pltpu.make_async_remote_copy(
            src_ref=source.at[buffer_at],
            dst_ref=target.at[out_at],
            send_sem=send.at[d],
            recv_sem=recv.at[d],
            device_id={"wave": lax.rem(me + d + 1, n)},
            device_id_type=MESH,
        )

    def first(d):
        return wave_copy(msg, recv1, ss1, rs1, d, lax.rem(me + d + 1, n), me)

    each(n - 1, lambda d: first(d).start())

    halos = (
        ("wave", me, n, 1, 0),
        ("wave", me, n, -1, 1),
        ("lev", lev, levels, 1, 2),
        ("lev", lev, levels, -1, 3),
    )

    def halo_copy(axis, place, step, k):
        return pltpu.make_async_remote_copy(
            src_ref=qs,
            dst_ref=qn.at[k],
            send_sem=ssq.at[k],
            recv_sem=rsq.at[k],
            device_id={axis: place + step},
            device_id_type=MESH,
        )

    def sends(place, count, step):
        return place < count - 1 if step > 0 else place > 0

    for axis, place, count, step, k in halos:

        @pl.when(sends(place, count, step))
        def _():
            halo_copy(axis, place, step, k).start()

    lane1 = lax.broadcasted_iota(jnp.int32, (1, wl), 1)
    target = lax.broadcasted_iota(jnp.int32, (wl, total_slots), 0)
    source_at = lax.broadcasted_iota(jnp.int32, (wl, total_slots), 1)
    column = jnp.sum(
        jnp.where(source_at == lax.rem(target, n) * slots + target // n, owner, 0.0),
        axis=1,
        keepdims=True,
    )
    square = (wl, wl)
    diagonal = lax.broadcasted_iota(jnp.int32, square, 0) == lax.broadcasted_iota(jnp.int32, square, 1)
    numbers = jnp.sum(jnp.where(diagonal, column, 0.0), axis=0, keepdims=True)
    filled = lane1 < slots * n
    block = 32 if length % 32 == 0 else 8 if length % 8 == 0 else length

    def table_block(b):
        start = b * block
        if not isinstance(b, int):
            start = pl.multiple_of(start, block)
        lon = lax.broadcasted_iota(jnp.int32, (block, wl), 0).astype(jnp.float32)
        if isinstance(b, int):
            lon = lon + float(start)
        else:
            lon = lon + start.astype(jnp.float32)
        product = numbers * lon
        turn = product - length * jnp.floor(product * (1.0 / length))
        turn = jnp.where(turn < 0, turn + length, turn)
        turn = jnp.where(turn >= length, turn - length, turn)
        turn = jnp.where(turn > length / 2, turn - length, turn)
        size = jnp.abs(turn)
        unit = 2.0 * math.pi / length
        cosine = small_sin((length / 4 - size) * unit)
        sine = small_sin(jnp.minimum(size, length / 2 - size) * unit)
        minus_sine = jnp.where(turn > 0, -sine, sine)
        for part, value in enumerate((cosine, minus_sine)):
            high, low = halves(jnp.where(filled, value, 0.0))
            at = (pl.ds(start, block), pl.ds(part * wl, wl))
            thigh[at] = high.astype(jnp.bfloat16)
            tlow[at] = low.astype(jnp.bfloat16)

    each(length // block, table_block)
    degree_row = lax.broadcasted_iota(jnp.int32, (lat, degrees), 1).astype(jnp.float32)
    masked = jnp.concatenate(
        [jnp.where(degree_row >= own_order[s : s + 1], leg_ref[s], 0.0) for s in range(slots)], axis=0
    )
    high, low = halves(masked)
    lhigh[...] = high.astype(jnp.bfloat16)
    llow[...] = low.astype(jnp.bfloat16)

    recv1[me] = msg[me]

    def first_wait(d):
        source = lax.rem(me - d - 1 + n, n)
        pltpu.make_async_remote_copy(
            src_ref=msg.at[0],
            dst_ref=recv1.at[source],
            send_sem=ss1.at[d],
            recv_sem=rs1.at[d],
            device_id={"wave": source},
            device_id_type=MESH,
        ).wait_recv()

    each(n - 1, first_wait)
    got = jnp.sum(recv1[...], axis=0)

    dmsg[0:1, :] = got[3:4] * thick
    dmsg[1:2, :] = got[7:8] * thick

    def mass(d):
        return pltpu.make_async_remote_copy(
            src_ref=dmsg,
            dst_ref=recvd.at[lev],
            send_sem=ssd.at[d],
            recv_sem=rsd.at[d],
            device_id={"lev": lev + d + 1},
            device_id_type=MESH,
        )

    def mass_start(d):
        @pl.when(lev + d + 1 < levels)
        def _():
            mass(d).start()

    each(levels - 1, mass_start)
    left = jnp.concatenate([got[0:4], got[4:8]], axis=1)
    grid = split_dot(left, thigh[...], tlow[...], ((1,), (1,)))
    q = qs[...]
    lon_step = 2.0 * math.pi / length
    lat_step = math.pi / (slots * n)
    flux = grid[0:1] * q
    ahead = jnp.concatenate([flux[:, 1:], flux[:, :1]], axis=1)
    behind = jnp.concatenate([flux[:, -1:], flux[:, :-1]], axis=1)
    zonal = (ahead - behind) * (1.0 / (2.0 * lon_step))

    for axis, place, count, step, k in halos:

        @pl.when(sends(place, count, -step))
        def _():
            halo_copy(axis, place, -step, k).wait_recv()

    merid = (grid[2:3] * qn[1] - grid[1:2] * qn[0]) * (1.0 / (2.0 * lat_step))
    sine = jnp.full((1, 1), sine_ref[0], jnp.float32)
    base = (zonal + merid) / (1.0 - sine * sine)
    layer = grid[3:4] * thick
    above = qn[2]
    below = qn[3]


    def mass_wait(d):
        @pl.when(lev - d - 1 >= 0)
        def _():
            pltpu.make_async_remote_copy(
                src_ref=dmsg,
                dst_ref=recvd.at[lev - d - 1],
                send_sem=ssd.at[d],
                recv_sem=rsd.at[d],
                device_id={"lev": lev - d - 1},
                device_id_type=MESH,
            ).wait_recv()

    each(levels - 1, mass_wait)
    higher = jnp.sum(recvd[...], axis=0)
    left = jnp.concatenate([higher[0:1], higher[1:2]], axis=1)
    prefix = split_dot(left, thigh[...], tlow[...], ((1,), (1,)))
    omega_bottom = -(prefix + layer)
    omega_top = -prefix
    vertical = (omega_bottom * (q + below) * 0.5 - omega_top * (above + q) * 0.5) / thick
    tendency = -jnp.full((1, 1), weight_ref[0], jnp.float32) * (base + vertical)

    spectra = split_dot(tendency, thigh[...], tlow[...], ((1,), (0,))) * (2.0 / length)
    half = n // 2
    lane2 = lax.broadcasted_iota(jnp.int32, (tracers, wl), 1)
    row_of = lax.rem(lane2, n)

    def packed(to):
        cosine = pltpu.roll(spectra[:, :wl], lax.rem(wl + me - to, wl), 1)
        sine = pltpu.roll(spectra[:, wl:], lax.rem(wl + lax.rem(me + half, n) - to, wl), 1)
        return jnp.where(row_of == me, cosine, sine)

    def second(d):
        return wave_copy(send2, recv2, ss2, rs2, d, d, me)

    def second_start(d):
        send2[d] = packed(lax.rem(me + d + 1, n))
        second(d).start()

    each(n - 1, second_start)
    recv2[me] = packed(me)

    def second_wait(d):
        source = lax.rem(me - d - 1 + n, n)
        pltpu.make_async_remote_copy(
            src_ref=send2.at[d],
            dst_ref=recv2.at[source],
            send_sem=ss2.at[d],
            recv_sem=rs2.at[d],
            device_id={"wave": source},
            device_id_type=MESH,
        ).wait_recv()

    each(n - 1, second_wait)

    def gather(i, held):
        got_cos, got_sin = held
        piece = recv2[i]
        return (
            jnp.where(row_of == i, piece, got_cos),
            jnp.where(row_of == (i + half) % n, piece, got_sin),
        )

    parts = (jnp.zeros((tracers, wl), jnp.float32),) * 2
    if n <= 16:
        for i in range(n):
            parts = gather(i, parts)
    else:
        parts = lax.fori_loop(0, n, gather, parts)
    got_cos, got_sin = parts
    got_sin = jnp.where(row_of < half, pltpu.roll(got_sin, wl - half, 1), pltpu.roll(got_sin, half, 1))
    gathered = jnp.concatenate([got_cos, got_sin], axis=0)
    lane3 = lax.broadcasted_iota(jnp.int32, (sp, wl), 1)
    sub3 = lax.broadcasted_iota(jnp.int32, (sp, wl), 0)
    own = (lane3 >= sub3 * n) & (lane3 < sub3 * n + n)
    blocks = []
    for c in range(tracers):
        for r in range(2):
            i = r * tracers + c
            blocks.append(jnp.where(own, gathered[i : i + 1], 0.0))
    left = jnp.concatenate(blocks, axis=0)[:, : slots * n]
    result = split_dot(left, lhigh[...], llow[...], ((1,), (0,)))
    for c in range(tracers):
        for r in range(2):
            at = (c * 2 + r) * sp
            out_ref[c, r, :, 0, :] = result[at : at + slots]

    each(n - 1, lambda d: first(d).wait_send())
    each(n - 1, lambda d: second(d).wait_send())
    for axis, place, count, step, k in halos:

        @pl.when(sends(place, count, step))
        def _():
            halo_copy(axis, place, step, k).wait_send()

    def mass_sent(d):
        @pl.when(lev + d + 1 < levels)
        def _():
            mass(d).wait_send()

    each(levels - 1, mass_sent)


def shards(vort_div, legendre, owner_map, lat_sine, quad_weight, thickness, tracers):
    slots, lat, degrees = legendre.shape
    count, own_levels, own_rows, length = tracers.shape
    n, levels = lax.axis_size("wave"), lax.axis_size("lev")
    assert own_levels == 1 and own_rows == 1 and lat == n and n % 2 == 0
    wl = up_to(slots * n, 128)
    nd = up_to(degrees, 128)
    sp = up_to(slots, 8)
    f32 = jnp.float32
    bf16 = jnp.bfloat16
    operands = (
        vort_div,
        legendre,
        owner_map.reshape(1, -1),
        lat_sine,
        quad_weight,
        thickness,
        tracers,
    )
    shapes = [
        ((4, sp, nd), f32),
        ((length, 2 * wl), bf16),
        ((length, 2 * wl), bf16),
        ((slots * lat, degrees), bf16),
        ((slots * lat, degrees), bf16),
        ((n, 8, wl), f32),
        ((n, 8, wl), f32),
        ((count, length), f32),
        ((4, count, length), f32),
        ((2, wl), f32),
        ((levels, 2, wl), f32),
        ((n - 1, count, wl), f32),
        ((n, count, wl), f32),
    ]
    dma = pltpu.SemaphoreType.DMA
    scratch_bytes = sum(4 * math.prod(shape) for shape, _ in shapes)
    result = pl.pallas_call(
        functools.partial(kernel, n, levels, (slots, lat, degrees, length, count)),
        out_shape=jax.ShapeDtypeStruct((count, 2, slots, 1, degrees), f32),
        in_specs=[
            pl.BlockSpec(memory_space=pltpu.SMEM if x.shape == (1,) else pltpu.VMEM) for x in operands
        ],
        out_specs=pl.BlockSpec(memory_space=pltpu.VMEM),
        scratch_shapes=[pltpu.VMEM(shape, kind) for shape, kind in shapes]
        + [dma((n - 1,)), dma((n - 1,)), dma((4,)), dma((4,))]
        + [dma((levels - 1,)), dma((levels - 1,)), dma((n - 1,)), dma((n - 1,))],
        compiler_params=pltpu.CompilerParams(
            collective_id=0,
            has_side_effects=True,
            vmem_limit_bytes=min(2 * scratch_bytes + (8 << 20), 60 << 20),
        ),
    )(*operands)
    return jnp.transpose(result, (0, 1, 3, 2, 4))


def solution(mesh):
    placed = (
        P(None, "lev", "wave", None),
        P("wave", None, None),
        P(),
        P("wave"),
        P("wave"),
        P("lev"),
        P(None, "lev", "wave", None),
    )
    return jax.shard_map(
        shards,
        mesh=mesh,
        in_specs=placed,
        out_specs=P(None, None, "lev", "wave", None),
        check_vma=False,
    )
```
